256 devices in a mesh: occ: 8 (over z_lo, y), aux: 32 (over x, z_hi, core).
Axes of the slice: x: 4, y: 4, z: 8 (z_hi: 4, z_lo: 2; z = z_hi * 2 + z_lo), core: 2. Of those that a mesh axis runs over, the one named last changes fastest.
Arguments:
- b_factors: bfloat16 [10752, 16, 2048], P('aux', 'occ'), may hold values from -0.25 to 0.25
- occ_energy: float32 [16], replicated, may hold values from -1.2 to -0.3
- vir_energy: float32 [2048], replicated, may hold values from 0.3 to 4
- slab_owner: int32 [32], replicated, may hold values from 0 to 31, each once
- pair_mask: int32 [8, 3, 32], P('occ'), may hold values from 0 to 1, as said below
Outputs:
- gamma: bfloat16 [10752, 16, 2048], P('aux', 'occ')
The draws below stay inside these ranges and needn't reach their ends.
Inputs may be any that keep to these rules, and one draw needn't show every extreme that they name: pair_mask[I, 1, s] is 1 everywhere; pair_mask[I, 0, s] equals pair_mask[I', 2, s] where I' is the block before I (cyclically).
All inputs are finite; a program needn't handle non-finite values.
Results may differ from the reference program's by a relative error of at most 0.0047.
Values may be sent and summed in bfloat16 or wider, within the bound.
A program may use at most 128 MiB of HBM per device.

```python
import math
import jax
import jax.numpy as jnp
from jax import lax

AUX = 10752
SLAB = 64
OCC_DEV = 2
OCC = 16
NSLAB = 32
VIR = 2048
N_OCC = 8


def draw_pair_mask(key, part):
    key = jax.random.fold_in(key, 7)
    thresholds = jax.random.randint(jax.random.fold_in(key, 1), (NSLAB,), 20, 90)
    rolled = jax.random.randint(jax.random.fold_in(key, 2), (N_OCC, NSLAB), 0, 100)
    links = (rolled < thresholds[None, :]).astype(jnp.int32)
    before = jnp.roll(links, 1, axis=0)
    return jnp.stack([before, jnp.ones_like(links), links], axis=1)


def levels(key, extent, cuts, low, high):
    def one(dim, shards_of):
        heights = jax.random.uniform(jax.random.fold_in(jax.random.fold_in(key, 6), dim), (shards_of,), jnp.float32, low / len(cuts), high / len(cuts))
        return jnp.repeat(jnp.exp(heights), extent[dim] // shards_of).reshape((-1,) + (1,) * (len(extent) - dim - 1))

    level = one(*cuts[0])
    for cut in cuts[1:]:
        level = level * one(*cut)
    return level


def gaussian(key, shape, width, reach, shards=(), dtype=jnp.bfloat16):
    loudness = levels(key, shape, shards, -0.22, 0.18) if shards else 1.0
    result = jax.random.normal(key, shape, jnp.float32) * width * loudness
    return jnp.minimum(jnp.maximum(result, -reach), reach).astype(dtype)


def setup_inputs(seed: int = 0) -> dict:
    splits = jax.random.split(jax.random.key(seed), 6)
    b_factors = gaussian(splits[0], (AUX, OCC, VIR), (0.45 * AUX ** -0.25), 0.25, ((0, 32), (1, 8)))
    occ_energy = jnp.clip(jax.random.uniform(splits[1], (OCC,), jnp.float32, -1.2, -0.3), -1.2, -0.3)
    vir_energy = jnp.clip(jnp.exp(jax.random.uniform(splits[2], (VIR,), jnp.float32, math.log(0.3), math.log(4.0))), 0.3, 4.0)
    slab_owner = jax.random.permutation(splits[3], NSLAB).astype(jnp.int32)
    pair_mask = draw_pair_mask(jax.random.fold_in(splits[5], 71), 0)
    return dict(b_factors=b_factors, occ_energy=occ_energy, vir_energy=vir_energy, slab_owner=slab_owner, pair_mask=pair_mask)


def slab_gamma(factors, eps_blocks, eps_slabs, pair_mask, slab_index):
    slab_panel = lax.dynamic_index_in_dim(factors, slab_index, 3, keepdims=False).astype(jnp.float32)
    eps_slab = lax.dynamic_index_in_dim(eps_slabs, slab_index, 0, keepdims=False)
    weights = lax.dynamic_index_in_dim(pair_mask, slab_index, 2, keepdims=False).astype(jnp.float32)
    gamma_total = jnp.zeros(slab_panel.shape, jnp.float32)
    for position, offset in enumerate((-1, 0, 1)):
        partner_panel = jnp.roll(slab_panel, -offset, axis=1)
        partner_eps = jnp.roll(eps_blocks, -offset, axis=0)
        coulomb = jnp.einsum("pnia,pnjb->nijab", slab_panel, partner_panel)
        denominator = (eps_slab[None, None, None, :, None] + eps_slab[None, None, None, None, :]
                       - eps_blocks[:, :, None, None, None] - partner_eps[:, None, :, None, None])
        amplitude = (2.0 * coulomb - jnp.swapaxes(coulomb, 3, 4)) / denominator
        amplitude = amplitude * weights[:, position][:, None, None, None, None]
        rounded = lax.optimization_barrier(amplitude.astype(jnp.bfloat16))
        gamma_total = gamma_total + jnp.einsum("nijab,pnjb->pnia", rounded.astype(jnp.float32), partner_panel)
    return gamma_total.astype(jnp.bfloat16)


def reference(b_factors, occ_energy, vir_energy, slab_owner, pair_mask):
    factors = b_factors.reshape(AUX, N_OCC, OCC_DEV, NSLAB, SLAB)
    eps_blocks = occ_energy.reshape(N_OCC, OCC_DEV)
    eps_slabs = vir_energy.reshape(NSLAB, SLAB)
    pieces = lax.map(lambda slab_index: slab_gamma(factors, eps_blocks, eps_slabs, pair_mask, slab_index), slab_owner)
    return jnp.transpose(pieces, (1, 2, 3, 0, 4)).reshape(AUX, OCC, NSLAB * SLAB)
```

```python
import functools

import jax
import jax.numpy as jnp
from jax import lax
from jax.experimental import pallas as pl
from jax.experimental.pallas import tpu as pltpu
from jax.sharding import PartitionSpec as P

SLAB = 64
LANES = 128
X, ZH, CORES = 4, 4, 2
HALF = 16
CHUNK = 4
PART = jnp.bfloat16
MESH = pl.DeviceIdType.MESH
VMEM = pltpu.VMEM


def low_half(shape):
    return lax.broadcasted_iota(jnp.int32, shape, len(shape) - 1) < SLAB


def regroup_kernel(slab_ref, raw_ref, out_ref, wide):
    rows = out_ref.shape[1]
    step = 512

    @pl.loop(0, raw_ref.shape[0] // step)
    def _(n):
        at = pl.ds(pl.multiple_of(n * step, step), step)
        wide[at, :] = raw_ref[at, :].astype(jnp.float32)

    @pl.loop(0, out_ref.shape[0])
    def _(k):
        slab = slab_ref[k]
        tile = slab // 2
        odd = (slab % 2) == 1
        first = wide[pl.ds(tile * 2, rows, stride=32), :]
        second = wide[pl.ds(tile * 2 + 1, rows, stride=32), :]
        left = low_half(first.shape)
        in_order = jnp.where(left, first, pltpu.roll(second, SLAB, 1))
        swapped = jnp.where(left, pltpu.roll(first, SLAB, 1), second)
        out_ref[k] = jnp.where(odd, swapped, in_order).astype(out_ref.dtype)


def regroup(raw, slab_owner, rows, slabs):
    return pl.pallas_call(
        regroup_kernel,
        out_shape=jax.ShapeDtypeStruct((slabs, rows, LANES), raw.dtype),
        in_specs=[pl.BlockSpec(memory_space=pltpu.SMEM), pl.BlockSpec(memory_space=VMEM)],
        out_specs=pl.BlockSpec(memory_space=VMEM),
        scratch_shapes=[VMEM(raw.shape, jnp.float32)],
        compiler_params=pltpu.CompilerParams(vmem_limit_bytes=40 << 20),
        name="regroup",
    )(slab_owner, raw)


def ungroup_kernel(gamma_ref, raw_ref, wide):
    rows = gamma_ref.shape[1]
    step = 512

    @pl.loop(0, gamma_ref.shape[0] // 2)
    def _(tile):
        even = gamma_ref[2 * tile].astype(jnp.float32)
        odd = gamma_ref[2 * tile + 1].astype(jnp.float32)
        left = low_half(even.shape)
        wide[pl.ds(tile * 2, rows, stride=32), :] = jnp.where(left, even, pltpu.roll(odd, SLAB, 1))
        wide[pl.ds(tile * 2 + 1, rows, stride=32), :] = jnp.where(
            left, pltpu.roll(even, SLAB, 1), odd
        )

    @pl.loop(0, raw_ref.shape[0] // step)
    def _(n):
        at = pl.ds(pl.multiple_of(n * step, step), step)
        raw_ref[at, :] = wide[at, :].astype(raw_ref.dtype)


def ungroup(gamma):
    slabs, rows, _ = gamma.shape
    shape = (slabs * rows, LANES)
    return pl.pallas_call(
        ungroup_kernel,
        out_shape=jax.ShapeDtypeStruct(shape, gamma.dtype),
        in_specs=[pl.BlockSpec(memory_space=VMEM)],
        out_specs=pl.BlockSpec(memory_space=VMEM),
        scratch_shapes=[VMEM(shape, jnp.float32)],
        compiler_params=pltpu.CompilerParams(vmem_limit_bytes=40 << 20),
        name="ungroup",
    )(gamma)


def dot(a, b, ca, cb):
    return lax.dot_general(a, b, (((ca,), (cb,)), ((), ())), preferred_element_type=jnp.float32)


def density_kernel(
    occ_count,
    slab_ref, occ_ref, mask_ref, vir_ref, own_ref,
    out_ref,
    panel, near, part, part_wide, part_in, total, lower_out, lower_in,
    unit_out, unit_in, amp, gamma_out,
    copy_sem, core_send, core_recv, halo_send, halo_recv, x_send, x_recv, y_send, y_recv,
    z_send, z_recv, low_send, low_recv, za_send, za_recv, zl_send, zl_recv,
    xa_send, xa_recv, out_send, out_recv,
):
    o = lax.axis_index("occ")
    aux = lax.axis_index("aux")
    core = aux % CORES
    zh = (aux // CORES) % ZH
    x = aux // (CORES * ZH)
    other = 1 - core

    def device(occ, x_at, z_at, core_at):
        return (occ, (x_at * ZH + z_at) * CORES + core_at)

    below = lax.rem(o + occ_count - 1, occ_count)
    above = lax.rem(o + 1, occ_count)
    x_peers = [lax.rem(x + d, X) for d in range(X)]
    z_peers = [lax.rem(zh + d, ZH) for d in range(ZH)]
    my_half, my_row = zh // 2, zh % 2

    def remote(src, dst, send, recv, to):
        return pltpu.make_async_remote_copy(
            src_ref=src, dst_ref=dst, send_sem=send, recv_sem=recv, device_id=to,
            device_id_type=MESH,
        )

    partners = [device(o, x, zh, other)]
    partners += [device(b, x, zh, c) for b in (below, above) for c in (0, 1)]
    partners += [device(o, x_peers[d], zh, core) for d in range(1, X)]
    partners += [device(o, x, z_peers[d], core) for d in range(1, ZH)]
    barrier = pltpu.get_barrier_semaphore()
    for partner in partners:
        pl.semaphore_signal(barrier, inc=1, device_id=partner, device_id_type=MESH)
    pl.semaphore_wait(barrier, len(partners))

    chunks = HALF // CHUNK

    def slabs_of(core_at, j):
        return own_ref.at[pl.ds(core_at * HALF + j * CHUNK, CHUNK)]

    def core_copy(j):
        return remote(
            slabs_of(other, j), panel.at[core, pl.ds(j * CHUNK, CHUNK)],
            core_send.at[j], core_recv.at[j], device(o, x, zh, other),
        )

    def halo_copy(n, core_at):
        phase, j = divmod(n, chunks)
        way = core if phase == 0 else other
        to = jnp.where(way == 0, below, above)
        return remote(
            slabs_of(core_at, j), near.at[way, core, pl.ds(j * CHUNK, CHUNK)],
            halo_send.at[n, core_at], halo_recv.at[n, way], device(to, x, zh, core_at),
        )

    def halo_start(n):
        for core_at in (0, 1):
            halo_copy(n, core_at).start()

    def halo_wait_send(n):
        for core_at in (0, 1):
            halo_copy(n, core_at).wait_send()

    def halo_wait_recv(n):
        phase, j = divmod(n, chunks)
        for way in (0, 1):
            source_core = way if phase == 0 else 1 - way
            landed = near.at[way, source_core, pl.ds(j * CHUNK, CHUNK)]
            remote(landed, landed, halo_send.at[n, 0], halo_recv.at[n, way],
                   device(above, x, zh, source_core)).wait_recv()

    local = pltpu.make_async_copy(
        own_ref.at[pl.ds(core * HALF, HALF)], panel.at[core], copy_sem
    )
    halo_start(0)
    local.start()
    core_copy(0).start()
    halo_start(1)
    for j in range(1, chunks):
        core_copy(j).start()
    local.wait()

    def part_copy(g, h, d):
        to = x_peers[d]
        return remote(part.at[g, h, to], part_in.at[g, h, d], x_send.at[g, h, d],
                      x_recv.at[g, h, d], device(o, to, zh, core))

    def coulomb(j):
        g, h = divmod(j, 2)

        @pl.loop(0, CHUNK)
        def _(s):
            q = j * CHUNK + s
            first, second = panel[0, q], panel[1, q]
            sums = (
                dot(first, first, 0, 0) + dot(second, second, 0, 0),
                dot(first, near[0, 0, q], 0, 0),
                dot(near[1, 1, q], second, 0, 0),
            )
            for m in range(3):
                part_wide[g, h, s, m] = sums[m]
                part[g, h, s, m] = sums[m].astype(PART)

        for d in range(1, X):
            part_copy(g, h, d).start()

    def lower_copy(g):
        return remote(lower_out.at[g], lower_in.at[g], y_send.at[g], y_recv.at[g],
                      device(below, x, zh, core))

    def add_over_x(g):
        for h in range(2):
            for d in range(1, X):
                part_copy(g, h, d).wait_recv()
        for h in range(2):
            for m in range(3):
                value = part_wide[g, h, x, m]
                for d in range(1, X):
                    value = value + part_in[g, h, d, m].astype(jnp.float32)
                if m < 2:
                    total[g, h, m] = value
                else:
                    lower_out[g, h] = value.astype(PART)
        lower_copy(g).start()

    def unit_copy(g, d):
        to = z_peers[d]
        return remote(unit_out.at[g, to], unit_in.at[g, d], z_send.at[g, d], z_recv.at[g, d],
                      device(o, x, to, core))

    def spread_over_z(g):
        lower_copy(g).wait_recv()
        for h in range(2):
            total[g, h, 1] = total[g, h, 1] + lower_in[g, h].astype(jnp.float32)
            for m in range(2):
                for i in range(2):
                    unit_out[g, 2 * h + i, m] = total[g, h, m, i * SLAB : (i + 1) * SLAB].astype(PART)
        for d in range(1, ZH):
            unit_copy(g, d).start()

    def amp_copy(g, d):
        mine = amp.at[g, my_half, x, pl.ds(0, 2), my_row]
        return remote(mine, mine, za_send.at[g, d], za_recv.at[g, d], device(o, x, z_peers[d], core))

    def amp_up_copy(g):
        return remote(amp.at[g, my_half, x, 1, my_row], amp.at[g, my_half, x, 2, my_row],
                      low_send.at[g], low_recv.at[g], device(above, x, zh, core))

    def amp_low_copy(g, d):
        mine = amp.at[g, my_half, x, 2, my_row]
        return remote(mine, mine, zl_send.at[g, d], zl_recv.at[g, d], device(o, x, z_peers[d], core))

    def amplitude(g):
        for d in range(1, ZH):
            unit_copy(g, d).wait_recv()
        row = pl.multiple_of(my_row * SLAB, SLAB)
        halves = []
        for m in range(2):
            value = total[g, my_half, m, pl.ds(row, SLAB), :]
            for d in range(1, ZH):
                value = value + unit_in[g, d, m].astype(jnp.float32)
            halves.append(value)
        whole = jnp.concatenate(halves, axis=0)
        turned = whole.T
        crossed = pltpu.roll(
            jnp.concatenate([turned[SLAB:], turned[:SLAB]], axis=0), SLAB, 1
        )
        square = (LANES, LANES)
        left = low_half(square)
        top = lax.broadcasted_iota(jnp.int32, square, 0) < SLAB
        swapped = jnp.where(left == top, turned, crossed)
        k = core * HALF + g * 2 * CHUNK + my_half * CHUNK + x
        slab = slab_ref[k]
        line = vir_ref[pl.ds(slab // 2, 1), :]
        flipped = pltpu.roll(line, SLAB, 1)
        take = low_half(line.shape) == ((slab % 2) == 0)
        eps_b = jnp.broadcast_to(jnp.where(take, line, flipped), square)
        eps_i = occ_ref[2 * o + my_row]
        eps_j = jnp.where(
            top,
            jnp.where(left, occ_ref[2 * o], occ_ref[2 * o + 1]),
            jnp.where(left, occ_ref[2 * above], occ_ref[2 * above + 1]),
        )
        denominator = eps_b.T + eps_b - eps_i - eps_j
        weight = jnp.where(top, mask_ref[0, 1, slab], mask_ref[0, 2, slab]).astype(jnp.float32)
        value = ((2.0 * whole - swapped) / denominator * weight).astype(amp.dtype)
        amp[g, my_half, x, 0, my_row] = value[:SLAB]
        amp[g, my_half, x, 1, my_row] = value[SLAB:]
        amp_up_copy(g).start()
        for d in range(1, ZH):
            amp_copy(g, d).start()

    def pass_lower(g):
        amp_up_copy(g).wait_recv()
        for d in range(1, ZH):
            amp_low_copy(g, d).start()

    def from_z(g, d):
        peer = z_peers[ZH - d]
        return g, peer // 2, x, peer % 2

    def panel_copy(g, d):
        mine = amp.at[g, pl.ds(0, 2), x]
        return remote(mine, mine, xa_send.at[g, d], xa_recv.at[g, d],
                      device(o, x_peers[d], zh, core))

    def gather_over_x(g):
        for d in range(1, ZH):
            at, half, x_at, row = from_z(g, d)
            landed = amp.at[at, half, x_at, pl.ds(0, 2), row]
            remote(landed, landed, za_send.at[g, d], za_recv.at[g, d],
                   device(o, x, z_peers[d], core)).wait_recv()
            landed = amp.at[at, half, x_at, 2, row]
            remote(landed, landed, zl_send.at[g, d], zl_recv.at[g, d],
                   device(o, x, z_peers[d], core)).wait_recv()
        for d in range(1, X):
            panel_copy(g, d).start()

    def amps_here(g):
        for d in range(1, X):
            landed = amp.at[g, pl.ds(0, 2), x_peers[X - d]]
            remote(landed, landed, xa_send.at[g, d], xa_recv.at[g, d],
                   device(o, x_peers[d], zh, core)).wait_recv()

    def gamma_copy(j):
        return remote(
            gamma_out.at[pl.ds(j * CHUNK, CHUNK)],
            out_ref.at[pl.ds(core * HALF + j * CHUNK, CHUNK)],
            out_send.at[j], out_recv.at[j], device(o, x, zh, other),
        )

    def density(j):
        g, h = divmod(j, 2)

        @pl.loop(0, CHUNK)
        def _(s):
            q = j * CHUNK + s
            own, up, low = (
                amp[g, h, s, m].reshape(LANES, LANES) for m in range(3)
            )

            def rows(at):
                value = dot(panel[at, q], own, 1, 1) + dot(near[0, at, q], up, 1, 1)
                return (value + dot(near[1, at, q], low, 1, 0)).astype(out_ref.dtype)

            gamma_out[q] = rows(other)
            out_ref[core * HALF + q] = rows(core)

        gamma_copy(j).start()

    for j in range(chunks):
        core_copy(j).wait_recv()
        halo_wait_recv(j)
        halo_wait_send(j)
        halo_start(j + 2)
        coulomb(j)
        if j == 2:
            add_over_x(0)
    spread_over_z(0)
    amplitude(0)
    pass_lower(0)
    add_over_x(1)
    halo_wait_send(4)
    halo_start(6)
    gather_over_x(0)
    spread_over_z(1)
    amplitude(1)
    halo_wait_send(5)
    halo_start(7)
    pass_lower(1)
    gather_over_x(1)
    amps_here(0)
    for j in range(chunks):
        if j == 2:
            amps_here(1)
        halo_wait_recv(chunks + j)
        density(j)

    for n in (6, 7):
        halo_wait_send(n)
    for j in range(chunks):
        core_copy(j).wait_send()
    for g in range(2):
        for h in range(2):
            for d in range(1, X):
                part_copy(g, h, d).wait_send()
        lower_copy(g).wait_send()
        amp_up_copy(g).wait_send()
        for d in range(1, ZH):
            unit_copy(g, d).wait_send()
            amp_copy(g, d).wait_send()
            amp_low_copy(g, d).wait_send()
        for d in range(1, X):
            panel_copy(g, d).wait_send()
    for j in range(chunks):
        gamma_copy(j).wait_send()
        landed = out_ref.at[pl.ds(other * HALF + j * CHUNK, CHUNK)]
        remote(landed, landed, out_send.at[j], out_recv.at[j],
               device(o, x, zh, other)).wait_recv()


def density(grouped, slab_owner, occ_energy, pair_mask, vir_energy):
    slabs, rows, _ = grouped.shape
    dma = pltpu.SemaphoreType.DMA
    bf16, f32 = jnp.bfloat16, jnp.float32
    smem, vmem = pl.BlockSpec(memory_space=pltpu.SMEM), pl.BlockSpec(memory_space=VMEM)
    halos = 2 * HALF // CHUNK
    return pl.pallas_call(
        functools.partial(density_kernel, lax.axis_size("occ")),
        out_shape=jax.ShapeDtypeStruct(grouped.shape, bf16),
        in_specs=[smem, smem, smem, vmem, vmem],
        out_specs=vmem,
        scratch_shapes=[
            VMEM((2, HALF, rows, LANES), bf16),
            VMEM((2, 2, HALF, rows, LANES), bf16),
            VMEM((2, 2, X, 3, LANES, LANES), PART),
            VMEM((2, 2, X, 3, LANES, LANES), f32),
            VMEM((2, 2, X, 3, LANES, LANES), PART),
            VMEM((2, 2, 2, LANES, LANES), f32),
            VMEM((2, 2, LANES, LANES), PART),
            VMEM((2, 2, LANES, LANES), PART),
            VMEM((2, ZH, 2, SLAB, LANES), PART),
            VMEM((2, ZH, 2, SLAB, LANES), PART),
            VMEM((2, 2, X, 3, 2, SLAB, LANES), bf16),
            VMEM((HALF, rows, LANES), bf16),
            dma, dma((4,)), dma((4,)), dma((halos, 2)), dma((halos, 2)),
            dma((2, 2, X)), dma((2, 2, X)), dma((2,)), dma((2,)),
            dma((2, ZH)), dma((2, ZH)), dma((2,)), dma((2,)),
            dma((2, ZH)), dma((2, ZH)), dma((2, ZH)), dma((2, ZH)),
            dma((2, X)), dma((2, X)), dma((4,)), dma((4,)),
        ],
        compiler_params=pltpu.CompilerParams(
            collective_id=0, has_side_effects=True, vmem_limit_bytes=56 << 20
        ),
        name="density",
    )(slab_owner, occ_energy, pair_mask, vir_energy, grouped)


def on_device(b_factors, occ_energy, vir_energy, slab_owner, pair_mask):
    aux_rows, occ_rows, virtuals = b_factors.shape
    tiles = virtuals // LANES
    raw = b_factors.reshape(aux_rows, occ_rows, tiles, LANES)
    raw = jnp.swapaxes(raw, 1, 2).reshape(aux_rows * tiles * occ_rows, LANES)
    grouped = regroup(raw, slab_owner, aux_rows, virtuals // SLAB)
    gamma = density(
        grouped, slab_owner, occ_energy, pair_mask, vir_energy.reshape(tiles, LANES)
    )
    raw = ungroup(gamma).reshape(aux_rows, tiles, occ_rows, LANES)
    return jnp.swapaxes(raw, 1, 2).reshape(aux_rows, occ_rows, virtuals)


def solution(mesh):
    placed = (P("aux", "occ", None), P(), P(), P(), P("occ", None, None))
    return jax.shard_map(
        on_device, mesh=mesh, in_specs=placed, out_specs=P("aux", "occ", None), check_vma=False
    )
```

```python
import functools

import jax
import jax.numpy as jnp
from jax import lax
from jax.experimental import pallas as pl
from jax.experimental.pallas import tpu as pltpu
from jax.sharding import PartitionSpec as P

SLAB = 64
LANES = 128
X, ZH, CORES = 4, 4, 2
HALF = 16
CHUNK = 4
PIECE = 2
AHEAD = 3
STEP = 16
PART = jnp.bfloat16
MESH = pl.DeviceIdType.MESH
VMEM = pltpu.VMEM


def low_half(shape):
    return lax.broadcasted_iota(jnp.int32, shape, len(shape) - 1) < SLAB


def regroup_kernel(slab_ref, raw_ref, out_ref, wide):
    rows = out_ref.shape[1]

    @pl.loop(0, rows // STEP)
    def _(n):
        at = pl.multiple_of(n * STEP * 32, STEP * 32)
        block = raw_ref[pl.ds(at, STEP * 32), :].astype(jnp.float32)
        wide[:, pl.ds(pl.multiple_of(n * STEP, STEP), STEP), :] = jnp.swapaxes(
            block.reshape(STEP, 32, LANES), 0, 1
        )

    @pl.loop(0, out_ref.shape[0])
    def _(k):
        slab = slab_ref[k]
        odd = slab % 2
        kept = wide[slab]
        moved = pltpu.roll(wide[slab + 1 - 2 * odd], SLAB, 1)
        lane = lax.broadcasted_iota(jnp.int32, kept.shape, 1)
        out_ref[k] = jnp.where(lane // SLAB == odd, kept, moved).astype(out_ref.dtype)


def regroup(raw, slab_owner, rows, slabs):
    return pl.pallas_call(
        regroup_kernel,
        out_shape=jax.ShapeDtypeStruct((slabs, rows, LANES), raw.dtype),
        in_specs=[pl.BlockSpec(memory_space=pltpu.SMEM), pl.BlockSpec(memory_space=VMEM)],
        out_specs=pl.BlockSpec(memory_space=VMEM),
        scratch_shapes=[VMEM((slabs, rows, LANES), jnp.float32)],
        compiler_params=pltpu.CompilerParams(vmem_limit_bytes=24 << 20),
        name="regroup",
    )(slab_owner, raw)


def ungroup_kernel(gamma_ref, raw_ref):
    slabs, rows, _ = gamma_ref.shape

    @pl.loop(0, rows // STEP)
    def _(n):
        at = pl.ds(pl.multiple_of(n * STEP, STEP), STEP)
        block = gamma_ref[:, at, :].astype(jnp.float32).reshape(slabs // 2, 2, STEP, LANES)
        even, odd = block[:, 0], block[:, 1]
        left = low_half(even.shape)
        moved = pltpu.roll(jnp.where(left, odd, even), SLAB, 2)
        pairs = jnp.stack([jnp.where(left, even, moved), jnp.where(left, moved, odd)], axis=1)
        lines = jnp.swapaxes(pairs.reshape(slabs, STEP, LANES), 0, 1)
        to = pl.ds(pl.multiple_of(n * STEP * 32, STEP * 32), STEP * 32)
        raw_ref[to, :] = lines.reshape(STEP * 32, LANES).astype(raw_ref.dtype)


def ungroup(gamma):
    slabs, rows, _ = gamma.shape
    return pl.pallas_call(
        ungroup_kernel,
        out_shape=jax.ShapeDtypeStruct((slabs * rows, LANES), gamma.dtype),
        in_specs=[pl.BlockSpec(memory_space=VMEM)],
        out_specs=pl.BlockSpec(memory_space=VMEM),
        compiler_params=pltpu.CompilerParams(vmem_limit_bytes=24 << 20),
        name="ungroup",
    )(gamma)


def dot(a, b, ca, cb):
    return lax.dot_general(a, b, (((ca,), (cb,)), ((), ())), preferred_element_type=jnp.float32)


def density_kernel(
    occ_count,
    slab_ref, occ_ref, mask_ref, vir_ref, own_ref,
    out_ref,
    panel, near, part, part_wide, part_in, total, unit_out, unit_in, low_in, amp, gamma_out,
    copy_sem, core_send, core_recv, halo_send, halo_recv, x_send, x_recv,
    z_send, z_recv, low_send, low_recv, za_send, za_recv, up_send, up_recv, zl_send, zl_recv,
    xa_send, xa_recv, out_send, out_recv,
):
    o = lax.axis_index("occ")
    aux = lax.axis_index("aux")
    core = aux % CORES
    zh = (aux // CORES) % ZH
    x = aux // (CORES * ZH)
    other = 1 - core

    def device(occ, x_at, z_at, core_at):
        return (occ, (x_at * ZH + z_at) * CORES + core_at)

    below = lax.rem(o + occ_count - 1, occ_count)
    above = lax.rem(o + 1, occ_count)
    x_peers = [lax.rem(x + d, X) for d in range(X)]
    z_peers = [lax.rem(zh + d, ZH) for d in range(ZH)]

    def remote(src, dst, send, recv, to):
        return pltpu.make_async_remote_copy(
            src_ref=src, dst_ref=dst, send_sem=send, recv_sem=recv, device_id=to,
            device_id_type=MESH,
        )

    def arrived(landed, recv, send):
        remote(landed, landed, send, recv, device(above, x, zh, core)).wait_recv()

    partners = [device(o, x, zh, other)]
    partners += [device(b, x, zh, c) for b in (below, above) for c in (0, 1)]
    partners += [device(o, x_peers[d], zh, core) for d in range(1, X)]
    partners += [device(o, x, z_peers[d], core) for d in range(1, ZH)]
    barrier = pltpu.get_barrier_semaphore()
    for partner in partners:
        pl.semaphore_signal(barrier, inc=1, device_id=partner, device_id_type=MESH)
    pl.semaphore_wait(barrier, len(partners))

    chunks = HALF // CHUNK

    def slabs_of(core_at, j):
        return own_ref.at[pl.ds(core_at * HALF + j * CHUNK, CHUNK)]

    def core_copy(j):
        return remote(
            slabs_of(other, j), panel.at[core, pl.ds(j * CHUNK, CHUNK)],
            core_send.at[j], core_recv.at[j], device(o, x, zh, other),
        )

    pieces = HALF // PIECE

    def halo_copy(n, core_at):
        phase, j = divmod(n, pieces)
        way = core if phase == 0 else other
        to = jnp.where(way == 0, below, above)
        return remote(
            own_ref.at[pl.ds(core_at * HALF + j * PIECE, PIECE)],
            near.at[way, core, pl.ds(j * PIECE, PIECE)],
            halo_send.at[n, core_at], halo_recv.at[n, way], device(to, x, zh, core_at),
        )

    def halo_start(n):
        for core_at in (0, 1):
            halo_copy(n, core_at).start()

    def halo_wait_send(n):
        for core_at in (0, 1):
            halo_copy(n, core_at).wait_send()

    def halo_wait_recv(n):
        phase, j = divmod(n, pieces)
        for way in (0, 1):
            source_core = way if phase == 0 else 1 - way
            arrived(near.at[way, source_core, pl.ds(j * PIECE, PIECE)],
                    halo_recv.at[n, way], halo_send.at[n, 0])

    def part_copy(g, d):
        to = x_peers[d]
        return remote(part.at[g, to], part_in.at[g, d], x_send.at[g, d], x_recv.at[g, d],
                      device(o, to, zh, core))

    def coulomb(g, half):
        @pl.loop(half * PIECE, half * PIECE + PIECE)
        def _(s):
            q = g * CHUNK + s
            first, second = panel[0, q], panel[1, q]
            sums = (
                dot(first, first, 0, 0) + dot(second, second, 0, 0),
                dot(first, near[0, 0, q], 0, 0),
                dot(near[1, 1, q], second, 0, 0),
            )
            for m in range(3):
                part_wide[g, s, m] = sums[m]
                part[g, s, m] = sums[m].astype(PART)

        for d in range(1, X):

            @pl.when(x_peers[d] // PIECE == half)
            def _(d=d):
                part_copy(g, d).start()

    def unit_copy(g, d):
        to = z_peers[d]
        return remote(unit_out.at[g, to], unit_in.at[g, d], z_send.at[g, d], z_recv.at[g, d],
                      device(o, x, to, core))

    def unit_start(g, m):
        for d in range(1, ZH):

            @pl.when(z_peers[d] // 2 == m)
            def _(d=d):
                unit_copy(g, d).start()

    def low_copy(g):
        return remote(unit_out.at[g, pl.ds(4, 2)], low_in.at[g], low_send.at[g], low_recv.at[g],
                      device(below, x, zh, core))

    def add_over_x(g):
        for d in range(1, X):
            part_copy(g, d).wait_recv()
        for m in (2, 0, 1):
            value = part_wide[g, x, m]
            for d in range(1, X):
                value = value + part_in[g, d, m].astype(jnp.float32)
            for i in range(2):
                half = value[i * SLAB : (i + 1) * SLAB]
                if m < 2:
                    total[g, 2 * m + i] = half
                if m != 1:
                    unit_out[g, 2 * m + i] = half.astype(PART)
            if m == 2:
                low_copy(g).start()
        unit_start(g, 0)

    def add_low(g):
        low_copy(g).wait_recv()
        for i in range(2):
            value = total[g, 2 + i] + low_in[g, i].astype(jnp.float32)
            total[g, 2 + i] = value
            unit_out[g, 2 + i] = value.astype(PART)
        unit_start(g, 1)

    def amp_copy(g, d):
        mine = amp.at[g * CHUNK + x, zh]
        return remote(mine, mine, za_send.at[g, d], za_recv.at[g, d], device(o, x, z_peers[d], core))

    def amp_up_copy(g):
        q = g * CHUNK + x
        return remote(amp.at[q, zh], amp.at[q, zh + 2], up_send.at[g], up_recv.at[g],
                      device(above, x, zh, core))

    def amp_low_copy(g, d):
        mine = amp.at[g * CHUNK + x, zh + 2]
        return remote(mine, mine, zl_send.at[g, d], zl_recv.at[g, d], device(o, x, z_peers[d], core))

    def amplitude(g):
        for d in range(1, ZH):
            unit_copy(g, d).wait_recv()
        value = total[g, zh]
        for d in range(1, ZH):
            value = value + unit_in[g, d].astype(jnp.float32)
        turned = jnp.concatenate([value, value], axis=0).T
        left = low_half(value.shape)
        swapped = jnp.where(left, turned[:SLAB], turned[SLAB:])
        slab = slab_ref[core * HALF + g * CHUNK + x]
        line = vir_ref[pl.ds(slab // 2, 1), :]
        take = low_half(line.shape) == ((slab % 2) == 0)
        line = jnp.where(take, line, pltpu.roll(line, SLAB, 1))
        eps_b = jnp.broadcast_to(line, (LANES, LANES))
        block = jnp.where(zh < 2, o, above)
        eps_i = occ_ref[2 * o + zh % 2]
        eps_j = jnp.where(left, occ_ref[2 * block], occ_ref[2 * block + 1])
        denominator = eps_b.T[:SLAB] + eps_b[:SLAB] - eps_i - eps_j
        weight = mask_ref[0, 1 + zh // 2, slab].astype(jnp.float32)
        amp[g * CHUNK + x, zh] = (
            (2.0 * value - swapped) / denominator * weight
        ).astype(amp.dtype)

        @pl.when(zh >= 2)
        def _():
            amp_up_copy(g).start()

        for d in range(1, ZH):
            amp_copy(g, d).start()

    def pass_low(g):
        @pl.when(zh >= 2)
        def _():
            amp_up_copy(g).wait_recv()
            for d in range(1, ZH):
                amp_low_copy(g, d).start()

    def panel_copy(g, d):
        mine = amp.at[g * CHUNK + x]
        return remote(mine, mine, xa_send.at[g, d], xa_recv.at[g, d],
                      device(o, x_peers[d], zh, core))

    def gather_over_x(g):
        q = g * CHUNK + x
        for d in range(1, ZH):
            arrived(amp.at[q, z_peers[ZH - d]], za_recv.at[g, d], za_send.at[g, d])

            @pl.when(z_peers[ZH - d] >= 2)
            def _(d=d):
                arrived(amp.at[q, z_peers[ZH - d] + 2], zl_recv.at[g, d], zl_send.at[g, d])

        for d in range(1, X):
            panel_copy(g, d).start()

    def gamma_copy(j):
        return remote(
            gamma_out.at[pl.ds(j * PIECE, PIECE)],
            out_ref.at[pl.ds(core * HALF + j * PIECE, PIECE)],
            out_send.at[j], out_recv.at[j], device(o, x, zh, other),
        )

    def amps_here(g):
        for d in range(1, X):
            arrived(amp.at[g * CHUNK + x_peers[X - d]], xa_recv.at[g, d], xa_send.at[g, d])

    def density(j):
        @pl.loop(0, PIECE)
        def _(s):
            q = j * PIECE + s
            own, up, low = (
                amp[q, 2 * m : 2 * m + 2].reshape(LANES, LANES) for m in range(3)
            )

            def rows(at):
                value = dot(panel[at, q], own, 1, 1) + dot(near[0, at, q], up, 1, 1)
                return (value + dot(near[1, at, q], low, 1, 0)).astype(out_ref.dtype)

            gamma_out[q] = rows(other)
            out_ref[core * HALF + q] = rows(core)

        gamma_copy(j).start()

    local = pltpu.make_async_copy(
        own_ref.at[pl.ds(core * HALF, HALF)], panel.at[core], copy_sem
    )
    for n in range(AHEAD):
        halo_start(n)
        if n == 0:
            local.start()
            core_copy(0).start()
    for j in range(1, chunks):
        core_copy(j).start()
    local.wait()

    schedule = {n: [] for n in range(2 * pieces + 1)}
    for g in range(chunks):
        start = 2 * g
        last = g == chunks - 1
        schedule[start + 3].append((add_over_x, g))
        schedule[start + 4].append((add_low, g))
        schedule[start + (5 if last else 6)].append((amplitude, g))
        schedule[start + (6 if last else 7)].append((pass_low, g))
        schedule[start + 8].append((gather_over_x, g))
        schedule[start + 10].append((amps_here, g))
        schedule[start + 10].append((density, 2 * g))
        schedule[min(start + 11, 2 * pieces)].append((density, 2 * g + 1))
    for n in range(2 * pieces + 1):
        if n < 2 * pieces:
            if n < pieces and n % 2 == 0:
                core_copy(n // 2).wait_recv()
            halo_wait_recv(n)
            halo_wait_send(n)
            if n + AHEAD < 2 * pieces:
                halo_start(n + AHEAD)
            if n < pieces:
                coulomb(n // 2, n % 2)
        for stage, at in schedule[n]:
            stage(at)

    for j in range(pieces):
        gamma_copy(j).wait_send()
    for j in range(chunks):
        core_copy(j).wait_send()
        low_copy(j).wait_send()
        for d in range(1, X):
            part_copy(j, d).wait_send()
            panel_copy(j, d).wait_send()
        for d in range(1, ZH):
            unit_copy(j, d).wait_send()
            amp_copy(j, d).wait_send()

    @pl.when(zh >= 2)
    def _():
        for j in range(chunks):
            amp_up_copy(j).wait_send()
            for d in range(1, ZH):
                amp_low_copy(j, d).wait_send()

    for j in range(pieces):
        arrived(out_ref.at[pl.ds(other * HALF + j * PIECE, PIECE)], out_recv.at[j], out_send.at[j])


def density(grouped, slab_owner, occ_energy, pair_mask, vir_energy):
    slabs, rows, _ = grouped.shape
    dma = pltpu.SemaphoreType.DMA
    bf16, f32 = jnp.bfloat16, jnp.float32
    smem, vmem = pl.BlockSpec(memory_space=pltpu.SMEM), pl.BlockSpec(memory_space=VMEM)
    chunks, pieces = HALF // CHUNK, HALF // PIECE
    return pl.pallas_call(
        functools.partial(density_kernel, lax.axis_size("occ")),
        out_shape=jax.ShapeDtypeStruct(grouped.shape, bf16),
        in_specs=[smem, smem, smem, vmem, vmem],
        out_specs=vmem,
        scratch_shapes=[
            VMEM((2, HALF, rows, LANES), bf16),
            VMEM((2, 2, HALF, rows, LANES), bf16),
            VMEM((chunks, X, 3, LANES, LANES), PART),
            VMEM((chunks, X, 3, LANES, LANES), f32),
            VMEM((chunks, X, 3, LANES, LANES), PART),
            VMEM((chunks, ZH, SLAB, LANES), f32),
            VMEM((chunks, 6, SLAB, LANES), PART),
            VMEM((chunks, ZH, SLAB, LANES), PART),
            VMEM((chunks, 2, SLAB, LANES), PART),
            VMEM((HALF, 6, SLAB, LANES), bf16),
            VMEM((HALF, rows, LANES), bf16),
            dma, dma((chunks,)), dma((chunks,)), dma((2 * pieces, 2)), dma((2 * pieces, 2)),
            dma((chunks, X)), dma((chunks, X)),
            dma((chunks, ZH)), dma((chunks, ZH)), dma((chunks,)), dma((chunks,)),
            dma((chunks, ZH)), dma((chunks, ZH)), dma((chunks,)), dma((chunks,)),
            dma((chunks, ZH)), dma((chunks, ZH)),
            dma((chunks, X)), dma((chunks, X)), dma((pieces,)), dma((pieces,)),
        ],
        compiler_params=pltpu.CompilerParams(
            collective_id=0, has_side_effects=True, vmem_limit_bytes=36 << 20
        ),
        name="density",
    )(slab_owner, occ_energy, pair_mask, vir_energy, grouped)


def on_device(b_factors, occ_energy, vir_energy, slab_owner, pair_mask):
    aux_rows, occ_rows, virtuals = b_factors.shape
    tiles = virtuals // LANES
    raw = b_factors.reshape(aux_rows, occ_rows, tiles, LANES)
    raw = jnp.swapaxes(raw, 1, 2).reshape(aux_rows * tiles * occ_rows, LANES)
    grouped = regroup(raw, slab_owner, aux_rows, virtuals // SLAB)
    gamma = density(
        grouped, slab_owner, occ_energy, pair_mask, vir_energy.reshape(tiles, LANES)
    )
    raw = ungroup(gamma).reshape(aux_rows, tiles, occ_rows, LANES)
    return jnp.swapaxes(raw, 1, 2).reshape(aux_rows, occ_rows, virtuals)


def solution(mesh):
    placed = (P("aux", "occ", None), P(), P(), P(), P("occ", None, None))
    return jax.shard_map(
        on_device, mesh=mesh, in_specs=placed, out_specs=P("aux", "occ", None), check_vma=False
    )
```

```python
import functools

import jax
import jax.numpy as jnp
from jax import lax
from jax.experimental import pallas as pl
from jax.experimental.pallas import tpu as pltpu
from jax.sharding import PartitionSpec as P

SLAB = 64
LANES = 128
X, ZH, CORES = 4, 4, 2
HALF = 16
CHUNK = 4
PIECE = 2
AHEAD = 4
STEP = 16
PART = jnp.bfloat16
MESH = pl.DeviceIdType.MESH
VMEM = pltpu.VMEM


def low_half(shape):
    return lax.broadcasted_iota(jnp.int32, shape, len(shape) - 1) < SLAB


def regroup_kernel(slab_ref, raw_ref, out_ref, wide):
    rows = out_ref.shape[1]

    @pl.loop(0, rows // STEP)
    def _(n):
        at = pl.multiple_of(n * STEP * 32, STEP * 32)
        block = raw_ref[pl.ds(at, STEP * 32), :].astype(jnp.float32)
        wide[:, pl.ds(pl.multiple_of(n * STEP, STEP), STEP), :] = jnp.swapaxes(
            block.reshape(STEP, 32, LANES), 0, 1
        )

    @pl.loop(0, out_ref.shape[0])
    def _(k):
        slab = slab_ref[k]
        odd = slab % 2
        kept = wide[slab]
        moved = pltpu.roll(wide[slab + 1 - 2 * odd], SLAB, 1)
        lane = lax.broadcasted_iota(jnp.int32, kept.shape, 1)
        out_ref[k] = jnp.where(lane // SLAB == odd, kept, moved).astype(out_ref.dtype)


def regroup(raw, slab_owner, rows, slabs):
    return pl.pallas_call(
        regroup_kernel,
        out_shape=jax.ShapeDtypeStruct((slabs, rows, LANES), raw.dtype),
        in_specs=[pl.BlockSpec(memory_space=pltpu.SMEM), pl.BlockSpec(memory_space=VMEM)],
        out_specs=pl.BlockSpec(memory_space=VMEM),
        scratch_shapes=[VMEM((slabs, rows, LANES), jnp.float32)],
        compiler_params=pltpu.CompilerParams(vmem_limit_bytes=24 << 20),
        name="regroup",
    )(slab_owner, raw)


def ungroup_kernel(gamma_ref, raw_ref):
    slabs, rows, _ = gamma_ref.shape

    @pl.loop(0, rows // STEP)
    def _(n):
        at = pl.ds(pl.multiple_of(n * STEP, STEP), STEP)
        block = gamma_ref[:, at, :].astype(jnp.float32).reshape(slabs // 2, 2, STEP, LANES)
        even, odd = block[:, 0], block[:, 1]
        left = low_half(even.shape)
        moved = pltpu.roll(jnp.where(left, odd, even), SLAB, 2)
        pairs = jnp.stack([jnp.where(left, even, moved), jnp.where(left, moved, odd)], axis=1)
        lines = jnp.swapaxes(pairs.reshape(slabs, STEP, LANES), 0, 1)
        to = pl.ds(pl.multiple_of(n * STEP * 32, STEP * 32), STEP * 32)
        raw_ref[to, :] = lines.reshape(STEP * 32, LANES).astype(raw_ref.dtype)


def ungroup(gamma):
    slabs, rows, _ = gamma.shape
    return pl.pallas_call(
        ungroup_kernel,
        out_shape=jax.ShapeDtypeStruct((slabs * rows, LANES), gamma.dtype),
        in_specs=[pl.BlockSpec(memory_space=VMEM)],
        out_specs=pl.BlockSpec(memory_space=VMEM),
        compiler_params=pltpu.CompilerParams(vmem_limit_bytes=24 << 20),
        name="ungroup",
    )(gamma)


def dot(a, b, ca, cb):
    return lax.dot_general(a, b, (((ca,), (cb,)), ((), ())), preferred_element_type=jnp.float32)


def density_kernel(
    occ_count,
    slab_ref, occ_ref, mask_ref, vir_ref, own_ref,
    out_ref,
    panel, near, part, part_wide, part_in, total, unit_out, unit_in, low_in, amp, gamma_out,
    copy_sem, core_send, core_recv, halo_send, halo_recv, x_send, x_recv,
    z_send, z_recv, low_send, low_recv, za_send, za_recv, up_send, up_recv, zl_send, zl_recv,
    xa_send, xa_recv, out_send, out_recv,
):
    o = lax.axis_index("occ")
    aux = lax.axis_index("aux")
    core = aux % CORES
    zh = (aux // CORES) % ZH
    x = aux // (CORES * ZH)
    other = 1 - core

    def device(occ, x_at, z_at, core_at):
        return (occ, (x_at * ZH + z_at) * CORES + core_at)

    below = lax.rem(o + occ_count - 1, occ_count)
    above = lax.rem(o + 1, occ_count)
    x_peers = [lax.rem(x + d, X) for d in range(X)]
    z_peers = [lax.rem(zh + d, ZH) for d in range(ZH)]

    def remote(src, dst, send, recv, to):
        return pltpu.make_async_remote_copy(
            src_ref=src, dst_ref=dst, send_sem=send, recv_sem=recv, device_id=to,
            device_id_type=MESH,
        )

    def arrived(landed, recv, send):
        remote(landed, landed, send, recv, device(above, x, zh, core)).wait_recv()

    partners = [device(o, x, zh, other)]
    partners += [device(b, x, zh, c) for b in (below, above) for c in (0, 1)]
    partners += [device(o, x_peers[d], zh, core) for d in range(1, X)]
    partners += [device(o, x, z_peers[d], core) for d in range(1, ZH)]
    barrier = pltpu.get_barrier_semaphore()
    for partner in partners:
        pl.semaphore_signal(barrier, inc=1, device_id=partner, device_id_type=MESH)
    pl.semaphore_wait(barrier, len(partners))

    chunks = HALF // CHUNK

    def slabs_of(core_at, j):
        return own_ref.at[pl.ds(core_at * HALF + j * CHUNK, CHUNK)]

    def core_copy(j):
        return remote(
            slabs_of(other, j), panel.at[core, pl.ds(j * CHUNK, CHUNK)],
            core_send.at[j], core_recv.at[j], device(o, x, zh, other),
        )

    pieces = HALF // PIECE

    def halo_copy(n, core_at):
        phase, j = divmod(n, pieces)
        way = core if phase == 0 else other
        to = jnp.where(way == 0, below, above)
        return remote(
            own_ref.at[pl.ds(core_at * HALF + j * PIECE, PIECE)],
            near.at[way, core, pl.ds(j * PIECE, PIECE)],
            halo_send.at[n, core_at], halo_recv.at[n, way], device(to, x, zh, core_at),
        )

    halos = [(n, core_at) for n in range(2 * pieces) for core_at in (0, 1)]
    finished = []

    def advance():
        at = len(finished)
        if at < len(halos):
            halo_copy(*halos[at]).wait_send()
            finished.append(at)
            if at + AHEAD < len(halos):
                halo_copy(*halos[at + AHEAD]).start()

    def halo_wait_recv(n):
        phase, j = divmod(n, pieces)
        for way in (0, 1):
            source_core = way if phase == 0 else 1 - way
            arrived(near.at[way, source_core, pl.ds(j * PIECE, PIECE)],
                    halo_recv.at[n, way], halo_send.at[n, 0])

    def part_copy(g, d):
        to = x_peers[d]
        return remote(part.at[g, to], part_in.at[g, d], x_send.at[g, d], x_recv.at[g, d],
                      device(o, to, zh, core))

    def coulomb(g, half):
        @pl.loop(half * PIECE, half * PIECE + PIECE)
        def _(s):
            q = g * CHUNK + s
            first, second = panel[0, q], panel[1, q]
            sums = (
                dot(first, first, 0, 0) + dot(second, second, 0, 0),
                dot(first, near[0, 0, q], 0, 0),
                dot(near[1, 1, q], second, 0, 0),
            )
            for m in range(3):
                part_wide[g, s, m] = sums[m]
                part[g, s, m] = sums[m].astype(PART)

        for d in range(1, X):

            @pl.when(x_peers[d] // PIECE == half)
            def _(d=d):
                part_copy(g, d).start()

    def unit_copy(g, d):
        to = z_peers[d]
        return remote(unit_out.at[g, to], unit_in.at[g, d], z_send.at[g, d], z_recv.at[g, d],
                      device(o, x, to, core))

    def unit_start(g, m):
        for d in range(1, ZH):

            @pl.when(z_peers[d] // 2 == m)
            def _(d=d):
                unit_copy(g, d).start()

    def low_copy(g):
        return remote(unit_out.at[g, pl.ds(4, 2)], low_in.at[g], low_send.at[g], low_recv.at[g],
                      device(below, x, zh, core))

    def add_over_x(g):
        for d in range(1, X):
            part_copy(g, d).wait_recv()
        for m in (2, 0, 1):
            value = part_wide[g, x, m]
            for d in range(1, X):
                value = value + part_in[g, d, m].astype(jnp.float32)
            for i in range(2):
                half = value[i * SLAB : (i + 1) * SLAB]
                if m < 2:
                    total[g, 2 * m + i] = half
                if m != 1:
                    unit_out[g, 2 * m + i] = half.astype(PART)
            if m == 2:
                low_copy(g).start()
        unit_start(g, 0)

    def add_low(g):
        low_copy(g).wait_recv()
        for i in range(2):
            value = total[g, 2 + i] + low_in[g, i].astype(jnp.float32)
            total[g, 2 + i] = value
            unit_out[g, 2 + i] = value.astype(PART)
        unit_start(g, 1)

    def amp_copy(g, d):
        mine = amp.at[g * CHUNK + x, zh]
        return remote(mine, mine, za_send.at[g, d], za_recv.at[g, d], device(o, x, z_peers[d], core))

    def amp_up_copy(g):
        q = g * CHUNK + x
        return remote(amp.at[q, zh], amp.at[q, zh + 2], up_send.at[g], up_recv.at[g],
                      device(above, x, zh, core))

    def amp_low_copy(g, d):
        mine = amp.at[g * CHUNK + x, zh + 2]
        return remote(mine, mine, zl_send.at[g, d], zl_recv.at[g, d], device(o, x, z_peers[d], core))

    def amplitude(g):
        for d in range(1, ZH):
            unit_copy(g, d).wait_recv()
        value = total[g, zh]
        for d in range(1, ZH):
            value = value + unit_in[g, d].astype(jnp.float32)
        turned = jnp.concatenate([value, value], axis=0).T
        left = low_half(value.shape)
        swapped = jnp.where(left, turned[:SLAB], turned[SLAB:])
        slab = slab_ref[core * HALF + g * CHUNK + x]
        line = vir_ref[pl.ds(slab // 2, 1), :]
        take = low_half(line.shape) == ((slab % 2) == 0)
        line = jnp.where(take, line, pltpu.roll(line, SLAB, 1))
        eps_b = jnp.broadcast_to(line, (LANES, LANES))
        block = jnp.where(zh < 2, o, above)
        eps_i = occ_ref[2 * o + zh % 2]
        eps_j = jnp.where(left, occ_ref[2 * block], occ_ref[2 * block + 1])
        denominator = eps_b.T[:SLAB] + eps_b[:SLAB] - eps_i - eps_j
        weight = mask_ref[0, 1 + zh // 2, slab].astype(jnp.float32)
        amp[g * CHUNK + x, zh] = (
            (2.0 * value - swapped) / denominator * weight
        ).astype(amp.dtype)

        @pl.when(zh >= 2)
        def _():
            amp_up_copy(g).start()

        for d in range(1, ZH):
            amp_copy(g, d).start()

    def pass_low(g):
        @pl.when(zh >= 2)
        def _():
            amp_up_copy(g).wait_recv()
            for d in range(1, ZH):
                amp_low_copy(g, d).start()

    def panel_copy(g, d):
        mine = amp.at[g * CHUNK + x]
        return remote(mine, mine, xa_send.at[g, d], xa_recv.at[g, d],
                      device(o, x_peers[d], zh, core))

    def gather_over_x(g):
        q = g * CHUNK + x
        for d in range(1, ZH):
            arrived(amp.at[q, z_peers[ZH - d]], za_recv.at[g, d], za_send.at[g, d])

            @pl.when(z_peers[ZH - d] >= 2)
            def _(d=d):
                arrived(amp.at[q, z_peers[ZH - d] + 2], zl_recv.at[g, d], zl_send.at[g, d])

        for d in range(1, X):
            panel_copy(g, d).start()

    def gamma_copy(j):
        return remote(
            gamma_out.at[pl.ds(j * PIECE, PIECE)],
            out_ref.at[pl.ds(core * HALF + j * PIECE, PIECE)],
            out_send.at[j], out_recv.at[j], device(o, x, zh, other),
        )

    def amps_here(g):
        for d in range(1, X):
            arrived(amp.at[g * CHUNK + x_peers[X - d]], xa_recv.at[g, d], xa_send.at[g, d])

    def density(j):
        @pl.loop(0, PIECE)
        def _(s):
            q = j * PIECE + s
            own, up, low = (
                amp[q, 2 * m : 2 * m + 2].reshape(LANES, LANES) for m in range(3)
            )

            def rows(at):
                value = dot(panel[at, q], own, 1, 1) + dot(near[0, at, q], up, 1, 1)
                return (value + dot(near[1, at, q], low, 1, 0)).astype(out_ref.dtype)

            gamma_out[q] = rows(other)
            out_ref[core * HALF + q] = rows(core)

        gamma_copy(j).start()

    local = pltpu.make_async_copy(
        own_ref.at[pl.ds(core * HALF, HALF)], panel.at[core], copy_sem
    )
    for at in range(AHEAD):
        halo_copy(*halos[at]).start()
    local.start()
    core_copy(0).start()
    for j in range(1, chunks):
        core_copy(j).start()
    local.wait()

    steps = ((2, 3, 4, 5, 6, 8), (4, 5, 6, 7, 8, 10), (6, 7, 8, 9, 10, 12), (8, 9, 10, 11, 12, 14))
    schedule = {n: [] for n in range(2 * pieces + 1)}
    for at, stage in enumerate((add_over_x, add_low, amplitude, pass_low, gather_over_x, amps_here)):
        for g in range(chunks):
            schedule[steps[g][at]].append((stage, g))
    for g in range(chunks):
        for j in range(2):
            ready = max(steps[g][5], pieces + 2 * g + j)
            schedule[ready].append((density, 2 * g + j))
    for n in range(2 * pieces + 1):
        if n < 2 * pieces:
            if n < pieces and n % 2 == 0:
                core_copy(n // 2).wait_recv()
            halo_wait_recv(n)
            advance()
            if n < pieces:
                coulomb(n // 2, n % 2)
        stages = list(schedule[n])
        for stage, at in stages[: len(stages) // 2]:
            stage(at)
        advance()
        for stage, at in stages[len(stages) // 2 :]:
            stage(at)

    for j in range(pieces):
        gamma_copy(j).wait_send()
    for j in range(chunks):
        core_copy(j).wait_send()
        low_copy(j).wait_send()
        for d in range(1, X):
            part_copy(j, d).wait_send()
            panel_copy(j, d).wait_send()
        for d in range(1, ZH):
            unit_copy(j, d).wait_send()
            amp_copy(j, d).wait_send()

    @pl.when(zh >= 2)
    def _():
        for j in range(chunks):
            amp_up_copy(j).wait_send()
            for d in range(1, ZH):
                amp_low_copy(j, d).wait_send()

    for j in range(pieces):
        arrived(out_ref.at[pl.ds(other * HALF + j * PIECE, PIECE)], out_recv.at[j], out_send.at[j])


def density(grouped, slab_owner, occ_energy, pair_mask, vir_energy):
    slabs, rows, _ = grouped.shape
    dma = pltpu.SemaphoreType.DMA
    bf16, f32 = jnp.bfloat16, jnp.float32
    smem, vmem = pl.BlockSpec(memory_space=pltpu.SMEM), pl.BlockSpec(memory_space=VMEM)
    chunks, pieces = HALF // CHUNK, HALF // PIECE
    return pl.pallas_call(
        functools.partial(density_kernel, lax.axis_size("occ")),
        out_shape=jax.ShapeDtypeStruct(grouped.shape, bf16),
        in_specs=[smem, smem, smem, vmem, vmem],
        out_specs=vmem,
        scratch_shapes=[
            VMEM((2, HALF, rows, LANES), bf16),
            VMEM((2, 2, HALF, rows, LANES), bf16),
            VMEM((chunks, X, 3, LANES, LANES), PART),
            VMEM((chunks, X, 3, LANES, LANES), f32),
            VMEM((chunks, X, 3, LANES, LANES), PART),
            VMEM((chunks, ZH, SLAB, LANES), f32),
            VMEM((chunks, 6, SLAB, LANES), PART),
            VMEM((chunks, ZH, SLAB, LANES), PART),
            VMEM((chunks, 2, SLAB, LANES), PART),
            VMEM((HALF, 6, SLAB, LANES), bf16),
            VMEM((HALF, rows, LANES), bf16),
            dma, dma((chunks,)), dma((chunks,)), dma((2 * pieces, 2)), dma((2 * pieces, 2)),
            dma((chunks, X)), dma((chunks, X)),
            dma((chunks, ZH)), dma((chunks, ZH)), dma((chunks,)), dma((chunks,)),
            dma((chunks, ZH)), dma((chunks, ZH)), dma((chunks,)), dma((chunks,)),
            dma((chunks, ZH)), dma((chunks, ZH)),
            dma((chunks, X)), dma((chunks, X)), dma((pieces,)), dma((pieces,)),
        ],
        compiler_params=pltpu.CompilerParams(
            collective_id=0, has_side_effects=True, vmem_limit_bytes=36 << 20
        ),
        name="density",
    )(slab_owner, occ_energy, pair_mask, vir_energy, grouped)


def on_device(b_factors, occ_energy, vir_energy, slab_owner, pair_mask):
    aux_rows, occ_rows, virtuals = b_factors.shape
    tiles = virtuals // LANES
    raw = b_factors.reshape(aux_rows, occ_rows, tiles, LANES)
    raw = jnp.swapaxes(raw, 1, 2).reshape(aux_rows * tiles * occ_rows, LANES)
    grouped = regroup(raw, slab_owner, aux_rows, virtuals // SLAB)
    gamma = density(
        grouped, slab_owner, occ_energy, pair_mask, vir_energy.reshape(tiles, LANES)
    )
    raw = ungroup(gamma).reshape(aux_rows, tiles, occ_rows, LANES)
    return jnp.swapaxes(raw, 1, 2).reshape(aux_rows, occ_rows, virtuals)


def solution(mesh):
    placed = (P("aux", "occ", None), P(), P(), P(), P("occ", None, None))
    return jax.shard_map(
        on_device, mesh=mesh, in_specs=placed, out_specs=P("aux", "occ", None), check_vma=False
    )
```

```python
import functools

import jax
import jax.numpy as jnp
from jax import lax
from jax.experimental import pallas as pl
from jax.experimental.pallas import tpu as pltpu
from jax.sharding import PartitionSpec as P

SLAB = 64
LANES = 128
X, ZH, CORES = 4, 4, 2
HALF = 16
CHUNK = 4
PIECE = 2
AHEAD = 4
STEP = 16
PART = jnp.bfloat16
MESH = pl.DeviceIdType.MESH
VMEM = pltpu.VMEM


def low_half(shape):
    return lax.broadcasted_iota(jnp.int32, shape, len(shape) - 1) < SLAB


def split_rows(raw_ref, wide):
    @pl.loop(0, wide.shape[1] // STEP)
    def _(n):
        at = pl.multiple_of(n * STEP * 32, STEP * 32)
        block = raw_ref[pl.ds(at, STEP * 32), :].astype(jnp.float32)
        wide[:, pl.ds(pl.multiple_of(n * STEP, STEP), STEP), :] = jnp.swapaxes(
            block.reshape(STEP, 32, LANES), 0, 1
        )


def slab_panel(slab, wide):
    odd = slab % 2
    kept = wide[slab]
    moved = pltpu.roll(wide[slab + 1 - 2 * odd], SLAB, 1)
    lane = lax.broadcasted_iota(jnp.int32, kept.shape, 1)
    return jnp.where(lane // SLAB == odd, kept, moved).astype(jnp.bfloat16)


def ungroup_kernel(gamma_ref, raw_ref):
    slabs, rows, _ = gamma_ref.shape

    @pl.loop(0, rows // STEP)
    def _(n):
        at = pl.ds(pl.multiple_of(n * STEP, STEP), STEP)
        block = gamma_ref[:, at, :].astype(jnp.float32).reshape(slabs // 2, 2, STEP, LANES)
        even, odd = block[:, 0], block[:, 1]
        left = low_half(even.shape)
        moved = pltpu.roll(jnp.where(left, odd, even), SLAB, 2)
        pairs = jnp.stack([jnp.where(left, even, moved), jnp.where(left, moved, odd)], axis=1)
        lines = jnp.swapaxes(pairs.reshape(slabs, STEP, LANES), 0, 1)
        to = pl.ds(pl.multiple_of(n * STEP * 32, STEP * 32), STEP * 32)
        raw_ref[to, :] = lines.reshape(STEP * 32, LANES).astype(raw_ref.dtype)


def ungroup(gamma):
    slabs, rows, _ = gamma.shape
    return pl.pallas_call(
        ungroup_kernel,
        out_shape=jax.ShapeDtypeStruct((slabs * rows, LANES), gamma.dtype),
        in_specs=[pl.BlockSpec(memory_space=VMEM)],
        out_specs=pl.BlockSpec(memory_space=VMEM),
        compiler_params=pltpu.CompilerParams(vmem_limit_bytes=24 << 20),
        name="ungroup",
    )(gamma)


def dot(a, b, ca, cb):
    return lax.dot_general(a, b, (((ca,), (cb,)), ((), ())), preferred_element_type=jnp.float32)


def density_kernel(
    occ_count,
    slab_ref, occ_ref, mask_ref, vir_ref, raw_ref,
    out_ref,
    own_ref, wide,
    panel, near, part, part_wide, part_in, total, unit_out, unit_in, low_in, amp, gamma_out,
    copy_sem, core_send, core_recv, halo_send, halo_recv, x_send, x_recv,
    z_send, z_recv, low_send, low_recv, za_send, za_recv, up_send, up_recv, zl_send, zl_recv,
    xa_send, xa_recv, out_send, out_recv,
):
    o = lax.axis_index("occ")
    aux = lax.axis_index("aux")
    core = aux % CORES
    zh = (aux // CORES) % ZH
    x = aux // (CORES * ZH)
    other = 1 - core

    def device(occ, x_at, z_at, core_at):
        return (occ, (x_at * ZH + z_at) * CORES + core_at)

    below = lax.rem(o + occ_count - 1, occ_count)
    above = lax.rem(o + 1, occ_count)
    x_peers = [lax.rem(x + d, X) for d in range(X)]
    z_peers = [lax.rem(zh + d, ZH) for d in range(ZH)]

    def remote(src, dst, send, recv, to):
        return pltpu.make_async_remote_copy(
            src_ref=src, dst_ref=dst, send_sem=send, recv_sem=recv, device_id=to,
            device_id_type=MESH,
        )

    def arrived(landed, recv, send):
        remote(landed, landed, send, recv, device(above, x, zh, core)).wait_recv()

    partners = [device(o, x, zh, other)]
    partners += [device(b, x, zh, c) for b in (below, above) for c in (0, 1)]
    partners += [device(o, x_peers[d], zh, core) for d in range(1, X)]
    partners += [device(o, x, z_peers[d], core) for d in range(1, ZH)]
    barrier = pltpu.get_barrier_semaphore()
    for partner in partners:
        pl.semaphore_signal(barrier, inc=1, device_id=partner, device_id_type=MESH)
    split_rows(raw_ref, wide)

    def regroup(first, last):
        @pl.loop(first, last)
        def _(q):
            for k in (q, HALF + q):
                own_ref[k] = slab_panel(slab_ref[k], wide)

    regroup(0, CHUNK)
    pl.semaphore_wait(barrier, len(partners))

    chunks = HALF // CHUNK

    def slabs_of(core_at, j):
        return own_ref.at[pl.ds(core_at * HALF + j * CHUNK, CHUNK)]

    def core_copy(j):
        return remote(
            slabs_of(other, j), panel.at[core, pl.ds(j * CHUNK, CHUNK)],
            core_send.at[j], core_recv.at[j], device(o, x, zh, other),
        )

    pieces = HALF // PIECE

    def halo_copy(n, core_at):
        phase, j = divmod(n, pieces)
        way = core if phase == 0 else other
        to = jnp.where(way == 0, below, above)
        return remote(
            own_ref.at[pl.ds(core_at * HALF + j * PIECE, PIECE)],
            near.at[way, core, pl.ds(j * PIECE, PIECE)],
            halo_send.at[n, core_at], halo_recv.at[n, way], device(to, x, zh, core_at),
        )

    halos = [(n, core_at) for n in range(2 * pieces) for core_at in (0, 1)]
    finished = []

    def advance():
        at = len(finished)
        if at < len(halos):
            halo_copy(*halos[at]).wait_send()
            finished.append(at)
            if at + AHEAD < len(halos):
                halo_copy(*halos[at + AHEAD]).start()

    def halo_wait_recv(n):
        phase, j = divmod(n, pieces)
        for way in (0, 1):
            source_core = way if phase == 0 else 1 - way
            arrived(near.at[way, source_core, pl.ds(j * PIECE, PIECE)],
                    halo_recv.at[n, way], halo_send.at[n, 0])

    def part_copy(g, d):
        to = x_peers[d]
        return remote(part.at[g, to], part_in.at[g, d], x_send.at[g, d], x_recv.at[g, d],
                      device(o, to, zh, core))

    def coulomb(g, half):
        @pl.loop(half * PIECE, half * PIECE + PIECE)
        def _(s):
            q = g * CHUNK + s
            first, second = panel[0, q], panel[1, q]
            sums = (
                dot(first, first, 0, 0) + dot(second, second, 0, 0),
                dot(first, near[0, 0, q], 0, 0),
                dot(near[1, 1, q], second, 0, 0),
            )
            for m in range(3):
                part_wide[g, s, m] = sums[m]
                part[g, s, m] = sums[m].astype(PART)

        for d in range(1, X):

            @pl.when(x_peers[d] // PIECE == half)
            def _(d=d):
                part_copy(g, d).start()

    def unit_copy(g, d):
        to = z_peers[d]
        return remote(unit_out.at[g, to], unit_in.at[g, d], z_send.at[g, d], z_recv.at[g, d],
                      device(o, x, to, core))

    def unit_start(g, m):
        for d in range(1, ZH):

            @pl.when(z_peers[d] // 2 == m)
            def _(d=d):
                unit_copy(g, d).start()

    def low_copy(g):
        return remote(unit_out.at[g, pl.ds(4, 2)], low_in.at[g], low_send.at[g], low_recv.at[g],
                      device(below, x, zh, core))

    def add_over_x(g):
        for d in range(1, X):
            part_copy(g, d).wait_recv()
        for m in (2, 0, 1):
            value = part_wide[g, x, m]
            for d in range(1, X):
                value = value + part_in[g, d, m].astype(jnp.float32)
            for i in range(2):
                half = value[i * SLAB : (i + 1) * SLAB]
                if m < 2:
                    total[g, 2 * m + i] = half
                if m != 1:
                    unit_out[g, 2 * m + i] = half.astype(PART)
            if m == 2:
                low_copy(g).start()
        unit_start(g, 0)

    def add_low(g):
        low_copy(g).wait_recv()
        for i in range(2):
            value = total[g, 2 + i] + low_in[g, i].astype(jnp.float32)
            total[g, 2 + i] = value
            unit_out[g, 2 + i] = value.astype(PART)
        unit_start(g, 1)

    def amp_copy(g, d):
        mine = amp.at[g * CHUNK + x, zh]
        return remote(mine, mine, za_send.at[g, d], za_recv.at[g, d], device(o, x, z_peers[d], core))

    def amp_up_copy(g):
        q = g * CHUNK + x
        return remote(amp.at[q, zh], amp.at[q, zh + 2], up_send.at[g], up_recv.at[g],
                      device(above, x, zh, core))

    def amp_low_copy(g, d):
        mine = amp.at[g * CHUNK + x, zh + 2]
        return remote(mine, mine, zl_send.at[g, d], zl_recv.at[g, d], device(o, x, z_peers[d], core))

    def amplitude(g):
        for d in range(1, ZH):
            unit_copy(g, d).wait_recv()
        value = total[g, zh]
        for d in range(1, ZH):
            value = value + unit_in[g, d].astype(jnp.float32)
        turned = jnp.concatenate([value, value], axis=0).T
        left = low_half(value.shape)
        swapped = jnp.where(left, turned[:SLAB], turned[SLAB:])
        slab = slab_ref[core * HALF + g * CHUNK + x]
        line = vir_ref[pl.ds(slab // 2, 1), :]
        take = low_half(line.shape) == ((slab % 2) == 0)
        line = jnp.where(take, line, pltpu.roll(line, SLAB, 1))
        eps_b = jnp.broadcast_to(line, (LANES, LANES))
        block = jnp.where(zh < 2, o, above)
        eps_i = occ_ref[2 * o + zh % 2]
        eps_j = jnp.where(left, occ_ref[2 * block], occ_ref[2 * block + 1])
        denominator = eps_b.T[:SLAB] + eps_b[:SLAB] - eps_i - eps_j
        weight = mask_ref[0, 1 + zh // 2, slab].astype(jnp.float32)
        amp[g * CHUNK + x, zh] = (
            (2.0 * value - swapped) / denominator * weight
        ).astype(amp.dtype)

        @pl.when(zh >= 2)
        def _():
            amp_up_copy(g).start()

        for d in range(1, ZH):
            amp_copy(g, d).start()

    def pass_low(g):
        @pl.when(zh >= 2)
        def _():
            amp_up_copy(g).wait_recv()
            for d in range(1, ZH):
                amp_low_copy(g, d).start()

    def panel_copy(g, d):
        mine = amp.at[g * CHUNK + x]
        return remote(mine, mine, xa_send.at[g, d], xa_recv.at[g, d],
                      device(o, x_peers[d], zh, core))

    def gather_over_x(g):
        q = g * CHUNK + x
        for d in range(1, ZH):
            arrived(amp.at[q, z_peers[ZH - d]], za_recv.at[g, d], za_send.at[g, d])

            @pl.when(z_peers[ZH - d] >= 2)
            def _(d=d):
                arrived(amp.at[q, z_peers[ZH - d] + 2], zl_recv.at[g, d], zl_send.at[g, d])

        for d in range(1, X):
            panel_copy(g, d).start()

    def gamma_copy(j):
        return remote(
            gamma_out.at[pl.ds(j * PIECE, PIECE)],
            out_ref.at[pl.ds(core * HALF + j * PIECE, PIECE)],
            out_send.at[j], out_recv.at[j], device(o, x, zh, other),
        )

    def amps_here(g):
        for d in range(1, X):
            arrived(amp.at[g * CHUNK + x_peers[X - d]], xa_recv.at[g, d], xa_send.at[g, d])

    def density(j):
        @pl.loop(0, PIECE)
        def _(s):
            q = j * PIECE + s
            own, up, low = (
                amp[q, 2 * m : 2 * m + 2].reshape(LANES, LANES) for m in range(3)
            )

            def rows(at):
                value = dot(panel[at, q], own, 1, 1) + dot(near[0, at, q], up, 1, 1)
                return (value + dot(near[1, at, q], low, 1, 0)).astype(out_ref.dtype)

            gamma_out[q] = rows(other)
            out_ref[core * HALF + q] = rows(core)

        gamma_copy(j).start()

    local = pltpu.make_async_copy(
        own_ref.at[pl.ds(core * HALF, HALF)], panel.at[core], copy_sem
    )
    for at in range(AHEAD):
        halo_copy(*halos[at]).start()
    core_copy(0).start()
    regroup(CHUNK, HALF)
    local.start()
    for j in range(1, chunks):
        core_copy(j).start()
    local.wait()

    steps = ((2, 3, 4, 5, 6, 8), (4, 5, 6, 7, 8, 10), (6, 7, 8, 9, 10, 12), (8, 9, 10, 11, 12, 14))
    schedule = {n: [] for n in range(2 * pieces + 1)}
    for at, stage in enumerate((add_over_x, add_low, amplitude, pass_low, gather_over_x, amps_here)):
        for g in range(chunks):
            schedule[steps[g][at]].append((stage, g))
    for g in range(chunks):
        for j in range(2):
            ready = max(steps[g][5], pieces + 2 * g + j)
            schedule[ready].append((density, 2 * g + j))
    for n in range(2 * pieces + 1):
        if n < 2 * pieces:
            if n < pieces and n % 2 == 0:
                core_copy(n // 2).wait_recv()
            halo_wait_recv(n)
            advance()
            if n < pieces:
                coulomb(n // 2, n % 2)
        stages = list(schedule[n])
        for stage, at in stages[: len(stages) // 2]:
            stage(at)
        advance()
        for stage, at in stages[len(stages) // 2 :]:
            stage(at)

    for j in range(pieces):
        gamma_copy(j).wait_send()
    for j in range(chunks):
        core_copy(j).wait_send()
        low_copy(j).wait_send()
        for d in range(1, X):
            part_copy(j, d).wait_send()
            panel_copy(j, d).wait_send()
        for d in range(1, ZH):
            unit_copy(j, d).wait_send()
            amp_copy(j, d).wait_send()

    @pl.when(zh >= 2)
    def _():
        for j in range(chunks):
            amp_up_copy(j).wait_send()
            for d in range(1, ZH):
                amp_low_copy(j, d).wait_send()

    for j in range(pieces):
        arrived(out_ref.at[pl.ds(other * HALF + j * PIECE, PIECE)], out_recv.at[j], out_send.at[j])


def density(raw, rows, slab_owner, occ_energy, pair_mask, vir_energy):
    slabs = raw.shape[0] // rows
    dma = pltpu.SemaphoreType.DMA
    bf16, f32 = jnp.bfloat16, jnp.float32
    smem, vmem = pl.BlockSpec(memory_space=pltpu.SMEM), pl.BlockSpec(memory_space=VMEM)
    chunks, pieces = HALF // CHUNK, HALF // PIECE
    return pl.pallas_call(
        functools.partial(density_kernel, lax.axis_size("occ")),
        out_shape=jax.ShapeDtypeStruct((slabs, rows, LANES), bf16),
        in_specs=[smem, smem, smem, vmem, vmem],
        out_specs=vmem,
        scratch_shapes=[
            VMEM((slabs, rows, LANES), bf16),
            VMEM((slabs, rows, LANES), f32),
            VMEM((2, HALF, rows, LANES), bf16),
            VMEM((2, 2, HALF, rows, LANES), bf16),
            VMEM((chunks, X, 3, LANES, LANES), PART),
            VMEM((chunks, X, 3, LANES, LANES), f32),
            VMEM((chunks, X, 3, LANES, LANES), PART),
            VMEM((chunks, ZH, SLAB, LANES), f32),
            VMEM((chunks, 6, SLAB, LANES), PART),
            VMEM((chunks, ZH, SLAB, LANES), PART),
            VMEM((chunks, 2, SLAB, LANES), PART),
            VMEM((HALF, 6, SLAB, LANES), bf16),
            VMEM((HALF, rows, LANES), bf16),
            dma, dma((chunks,)), dma((chunks,)), dma((2 * pieces, 2)), dma((2 * pieces, 2)),
            dma((chunks, X)), dma((chunks, X)),
            dma((chunks, ZH)), dma((chunks, ZH)), dma((chunks,)), dma((chunks,)),
            dma((chunks, ZH)), dma((chunks, ZH)), dma((chunks,)), dma((chunks,)),
            dma((chunks, ZH)), dma((chunks, ZH)),
            dma((chunks, X)), dma((chunks, X)), dma((pieces,)), dma((pieces,)),
        ],
        compiler_params=pltpu.CompilerParams(
            collective_id=0, has_side_effects=True, vmem_limit_bytes=36 << 20
        ),
        name="density",
    )(slab_owner, occ_energy, pair_mask, vir_energy, raw)


def on_device(b_factors, occ_energy, vir_energy, slab_owner, pair_mask):
    aux_rows, occ_rows, virtuals = b_factors.shape
    tiles = virtuals // LANES
    raw = b_factors.reshape(aux_rows, occ_rows, tiles, LANES)
    raw = jnp.swapaxes(raw, 1, 2).reshape(aux_rows * tiles * occ_rows, LANES)
    gamma = density(
        raw, aux_rows, slab_owner, occ_energy, pair_mask, vir_energy.reshape(tiles, LANES)
    )
    raw = ungroup(gamma).reshape(aux_rows, tiles, occ_rows, LANES)
    return jnp.swapaxes(raw, 1, 2).reshape(aux_rows, occ_rows, virtuals)


def solution(mesh):
    placed = (P("aux", "occ", None), P(), P(), P(), P("occ", None, None))
    return jax.shard_map(
        on_device, mesh=mesh, in_specs=placed, out_specs=P("aux", "occ", None), check_vma=False
    )
```

```python
import functools

import jax
import jax.numpy as jnp
from jax import lax
from jax.experimental import pallas as pl
from jax.experimental.pallas import tpu as pltpu
from jax.sharding import PartitionSpec as P

SLAB = 64
LANES = 128
X, ZH, CORES = 4, 4, 2
HALF = 16
CHUNK = 4
PIECE = 2
AHEAD = 4
STEP = 16
PART = jnp.bfloat16
MESH = pl.DeviceIdType.MESH
VMEM = pltpu.VMEM


def low_half(shape):
    return lax.broadcasted_iota(jnp.int32, shape, len(shape) - 1) < SLAB


def split_rows(raw_ref, wide):
    @pl.loop(0, wide.shape[1] // STEP)
    def _(n):
        at = pl.multiple_of(n * STEP * 32, STEP * 32)
        block = raw_ref[pl.ds(at, STEP * 32), :].astype(jnp.float32)
        wide[:, pl.ds(pl.multiple_of(n * STEP, STEP), STEP), :] = jnp.swapaxes(
            block.reshape(STEP, 32, LANES), 0, 1
        )


def slab_panel(slab, wide):
    odd = slab % 2
    kept = wide[slab]
    moved = pltpu.roll(wide[slab + 1 - 2 * odd], SLAB, 1)
    lane = lax.broadcasted_iota(jnp.int32, kept.shape, 1)
    return jnp.where(lane // SLAB == odd, kept, moved).astype(jnp.bfloat16)


def ungroup_kernel(gamma_in, out_ref, gamma_ref, raw_ref, load_sem, sem):
    slabs, rows, _ = gamma_ref.shape

    def lay_out(n):
        at = pl.ds(pl.multiple_of(n * STEP, STEP), STEP)
        block = gamma_ref[:, at, :].astype(jnp.float32).reshape(slabs // 2, 2, STEP, LANES)
        even, odd = block[:, 0], block[:, 1]
        left = low_half(even.shape)
        moved = pltpu.roll(jnp.where(left, odd, even), SLAB, 2)
        pairs = jnp.stack([jnp.where(left, even, moved), jnp.where(left, moved, odd)], axis=1)
        lines = jnp.swapaxes(pairs.reshape(slabs, STEP, LANES), 0, 1)
        to = pl.ds(pl.multiple_of(n * STEP * 32, STEP * 32), STEP * 32)
        raw_ref[to, :] = lines.reshape(STEP * 32, LANES).astype(raw_ref.dtype)

    shares = 3
    share = raw_ref.shape[0] // shares
    steps = rows // STEP // shares
    loads, stores = [], []
    for at in range(shares):
        part = pl.ds(at * steps * STEP, steps * STEP)
        loads.append(
            pltpu.make_async_copy(gamma_in.at[:, part], gamma_ref.at[:, part], load_sem.at[at])
        )
        loads[-1].start()
    for at in range(shares):
        loads[at].wait()
        pl.loop(at * steps, (at + 1) * steps)(lay_out)
        done = pl.ds(at * share, share)
        stores.append(pltpu.make_async_copy(raw_ref.at[done], out_ref.at[done], sem.at[at]))
        stores[-1].start()
    for store in stores:
        store.wait()


def ungroup(gamma):
    slabs, rows, _ = gamma.shape
    return pl.pallas_call(
        ungroup_kernel,
        out_shape=jax.ShapeDtypeStruct((slabs * rows, LANES), gamma.dtype),
        in_specs=[pl.BlockSpec(memory_space=pltpu.HBM)],
        out_specs=pl.BlockSpec(memory_space=pltpu.HBM),
        scratch_shapes=[
            VMEM(gamma.shape, gamma.dtype), VMEM((slabs * rows, LANES), gamma.dtype),
            pltpu.SemaphoreType.DMA((3,)), pltpu.SemaphoreType.DMA((3,)),
        ],
        compiler_params=pltpu.CompilerParams(vmem_limit_bytes=57 << 20),
        name="ungroup",
    )(gamma)


def dot(a, b, ca, cb):
    return lax.dot_general(a, b, (((ca,), (cb,)), ((), ())), preferred_element_type=jnp.float32)


def density_kernel(
    occ_count,
    slab_in, occ_in, mask_in, vir_in, raw_in,
    out_ref,
    slab_ref, occ_ref, mask_ref, vir_ref, raw_ref, load_sem,
    own_ref, wide,
    panel, near, part, part_wide, part_in, total, unit_out, unit_in, low_in, amp, gamma_out, gamma_own,
    copy_sem, core_send, core_recv, halo_send, halo_recv, x_send, x_recv,
    z_send, z_recv, low_send, low_recv, za_send, za_recv, up_send, up_recv, zl_send, zl_recv,
    xa_send, xa_recv, out_send, out_recv, store_sem,
):
    o = lax.axis_index("occ")
    aux = lax.axis_index("aux")
    core = aux % CORES
    zh = (aux // CORES) % ZH
    x = aux // (CORES * ZH)
    other = 1 - core

    def device(occ, x_at, z_at, core_at):
        return (occ, (x_at * ZH + z_at) * CORES + core_at)

    below = lax.rem(o + occ_count - 1, occ_count)
    above = lax.rem(o + 1, occ_count)
    x_peers = [lax.rem(x + d, X) for d in range(X)]
    z_peers = [lax.rem(zh + d, ZH) for d in range(ZH)]

    def remote(src, dst, send, recv, to):
        return pltpu.make_async_remote_copy(
            src_ref=src, dst_ref=dst, send_sem=send, recv_sem=recv, device_id=to,
            device_id_type=MESH,
        )

    def arrived(landed, recv, send):
        remote(landed, landed, send, recv, device(above, x, zh, core)).wait_recv()

    partners = [device(o, x, zh, other)]
    partners += [device(b, x, zh, c) for b in (below, above) for c in (0, 1)]
    partners += [device(o, x_peers[d], zh, core) for d in range(1, X)]
    partners += [device(o, x, z_peers[d], core) for d in range(1, ZH)]
    loads = [
        pltpu.make_async_copy(source, landing, load_sem.at[n])
        for n, (source, landing) in enumerate((
            (raw_in, raw_ref), (slab_in, slab_ref), (occ_in, occ_ref), (mask_in, mask_ref),
            (vir_in, vir_ref),
        ))
    ]
    for load in loads:
        load.start()
    barrier = pltpu.get_barrier_semaphore()
    for partner in partners:
        pl.semaphore_signal(barrier, inc=1, device_id=partner, device_id_type=MESH)
    for load in loads:
        load.wait()
    split_rows(raw_ref, wide)

    def regroup(first, last):
        @pl.loop(first, last)
        def _(q):
            for k in (q, HALF + q):
                own_ref[k] = slab_panel(slab_ref[k], wide)

    regroup(0, CHUNK)
    pl.semaphore_wait(barrier, len(partners))

    chunks = HALF // CHUNK

    def slabs_of(core_at, j):
        return own_ref.at[pl.ds(core_at * HALF + j * CHUNK, CHUNK)]

    def core_copy(j):
        return remote(
            slabs_of(other, j), panel.at[core, pl.ds(j * CHUNK, CHUNK)],
            core_send.at[j], core_recv.at[j], device(o, x, zh, other),
        )

    pieces = HALF // PIECE

    def halo_copy(n, core_at):
        phase, j = divmod(n, pieces)
        way = core if phase == 0 else other
        to = jnp.where(way == 0, below, above)
        return remote(
            own_ref.at[pl.ds(core_at * HALF + j * PIECE, PIECE)],
            near.at[way, core, pl.ds(j * PIECE, PIECE)],
            halo_send.at[n, core_at], halo_recv.at[n, way], device(to, x, zh, core_at),
        )

    halos = [(n, core_at) for n in range(2 * pieces) for core_at in (0, 1)]
    finished = []

    def advance():
        at = len(finished)
        if at < len(halos):
            halo_copy(*halos[at]).wait_send()
            finished.append(at)
            if at + AHEAD < len(halos):
                halo_copy(*halos[at + AHEAD]).start()

    def halo_wait_recv(n):
        phase, j = divmod(n, pieces)
        for way in (0, 1):
            source_core = way if phase == 0 else 1 - way
            arrived(near.at[way, source_core, pl.ds(j * PIECE, PIECE)],
                    halo_recv.at[n, way], halo_send.at[n, 0])

    def part_copy(g, d):
        to = x_peers[d]
        return remote(part.at[g, to], part_in.at[g, d], x_send.at[g, d], x_recv.at[g, d],
                      device(o, to, zh, core))

    def coulomb(g, half):
        @pl.loop(half * PIECE, half * PIECE + PIECE)
        def _(s):
            q = g * CHUNK + s
            first, second = panel[0, q], panel[1, q]
            sums = (
                dot(first, first, 0, 0) + dot(second, second, 0, 0),
                dot(first, near[0, 0, q], 0, 0),
                dot(near[1, 1, q], second, 0, 0),
            )
            for m in range(3):
                part_wide[g, s, m] = sums[m]
                part[g, s, m] = sums[m].astype(PART)

        for d in range(1, X):

            @pl.when(x_peers[d] // PIECE == half)
            def _(d=d):
                part_copy(g, d).start()

    def unit_copy(g, d):
        to = z_peers[d]
        return remote(unit_out.at[g, to], unit_in.at[g, d], z_send.at[g, d], z_recv.at[g, d],
                      device(o, x, to, core))

    def unit_start(g, m):
        for d in range(1, ZH):

            @pl.when(z_peers[d] // 2 == m)
            def _(d=d):
                unit_copy(g, d).start()

    def low_copy(g):
        return remote(unit_out.at[g, pl.ds(4, 2)], low_in.at[g], low_send.at[g], low_recv.at[g],
                      device(below, x, zh, core))

    def add_over_x(g):
        for d in range(1, X):
            part_copy(g, d).wait_recv()
        for m in (2, 0, 1):
            value = part_wide[g, x, m]
            for d in range(1, X):
                value = value + part_in[g, d, m].astype(jnp.float32)
            for i in range(2):
                half = value[i * SLAB : (i + 1) * SLAB]
                if m < 2:
                    total[g, 2 * m + i] = half
                if m != 1:
                    unit_out[g, 2 * m + i] = half.astype(PART)
            if m == 2:
                low_copy(g).start()
        unit_start(g, 0)

    def add_low(g):
        low_copy(g).wait_recv()
        for i in range(2):
            value = total[g, 2 + i] + low_in[g, i].astype(jnp.float32)
            total[g, 2 + i] = value
            unit_out[g, 2 + i] = value.astype(PART)
        unit_start(g, 1)

    def amp_copy(g, d):
        mine = amp.at[g * CHUNK + x, zh]
        return remote(mine, mine, za_send.at[g, d], za_recv.at[g, d], device(o, x, z_peers[d], core))

    def amp_up_copy(g):
        q = g * CHUNK + x
        return remote(amp.at[q, zh], amp.at[q, zh + 2], up_send.at[g], up_recv.at[g],
                      device(above, x, zh, core))

    def amp_low_copy(g, d):
        mine = amp.at[g * CHUNK + x, zh + 2]
        return remote(mine, mine, zl_send.at[g, d], zl_recv.at[g, d], device(o, x, z_peers[d], core))

    def amplitude(g):
        for d in range(1, ZH):
            unit_copy(g, d).wait_recv()
        value = total[g, zh]
        for d in range(1, ZH):
            value = value + unit_in[g, d].astype(jnp.float32)
        turned = jnp.concatenate([value, value], axis=0).T
        left = low_half(value.shape)
        swapped = jnp.where(left, turned[:SLAB], turned[SLAB:])
        slab = slab_ref[core * HALF + g * CHUNK + x]
        line = vir_ref[pl.ds(slab // 2, 1), :]
        take = low_half(line.shape) == ((slab % 2) == 0)
        line = jnp.where(take, line, pltpu.roll(line, SLAB, 1))
        eps_b = jnp.broadcast_to(line, (LANES, LANES))
        block = jnp.where(zh < 2, o, above)
        eps_i = occ_ref[2 * o + zh % 2]
        eps_j = jnp.where(left, occ_ref[2 * block], occ_ref[2 * block + 1])
        denominator = eps_b.T[:SLAB] + eps_b[:SLAB] - eps_i - eps_j
        weight = mask_ref[1 + zh // 2, 0, slab].astype(jnp.float32)
        amp[g * CHUNK + x, zh] = (
            (2.0 * value - swapped) / denominator * weight
        ).astype(amp.dtype)

        @pl.when(zh >= 2)
        def _():
            amp_up_copy(g).start()

        for d in range(1, ZH):
            amp_copy(g, d).start()

    def pass_low(g):
        @pl.when(zh >= 2)
        def _():
            amp_up_copy(g).wait_recv()
            for d in range(1, ZH):
                amp_low_copy(g, d).start()

    def panel_copy(g, d):
        mine = amp.at[g * CHUNK + x]
        return remote(mine, mine, xa_send.at[g, d], xa_recv.at[g, d],
                      device(o, x_peers[d], zh, core))

    def gather_over_x(g):
        q = g * CHUNK + x
        for d in range(1, ZH):
            arrived(amp.at[q, z_peers[ZH - d]], za_recv.at[g, d], za_send.at[g, d])

            @pl.when(z_peers[ZH - d] >= 2)
            def _(d=d):
                arrived(amp.at[q, z_peers[ZH - d] + 2], zl_recv.at[g, d], zl_send.at[g, d])

        for d in range(1, X):
            panel_copy(g, d).start()

    def gamma_copy(j):
        return remote(
            gamma_out.at[pl.ds(j * PIECE, PIECE)],
            out_ref.at[pl.ds(core * HALF + j * PIECE, PIECE)],
            out_send.at[j], out_recv.at[j], device(o, x, zh, other),
        )

    def store(j):
        return pltpu.make_async_copy(
            gamma_own.at[pl.ds(j * PIECE, PIECE)],
            out_ref.at[pl.ds(core * HALF + j * PIECE, PIECE)], store_sem.at[j],
        )

    def amps_here(g):
        for d in range(1, X):
            arrived(amp.at[g * CHUNK + x_peers[X - d]], xa_recv.at[g, d], xa_send.at[g, d])

    def density(j):
        @pl.loop(0, PIECE)
        def _(s):
            q = j * PIECE + s
            own, up, low = (
                amp[q, 2 * m : 2 * m + 2].reshape(LANES, LANES) for m in range(3)
            )

            def rows(at):
                value = dot(panel[at, q], own, 1, 1) + dot(near[0, at, q], up, 1, 1)
                return (value + dot(near[1, at, q], low, 1, 0)).astype(out_ref.dtype)

            gamma_out[q] = rows(other)
            gamma_own[q] = rows(core)

        gamma_copy(j).start()
        store(j).start()

    local = pltpu.make_async_copy(
        own_ref.at[pl.ds(core * HALF, HALF)], panel.at[core], copy_sem
    )
    for at in range(AHEAD):
        halo_copy(*halos[at]).start()
    core_copy(0).start()
    regroup(CHUNK, HALF)
    local.start()
    for j in range(1, chunks):
        core_copy(j).start()
    local.wait()

    steps = ((2, 3, 4, 5, 6, 8), (4, 5, 6, 7, 8, 10), (6, 7, 8, 9, 10, 12), (8, 9, 10, 11, 12, 14))
    schedule = {n: [] for n in range(2 * pieces + 1)}
    for at, stage in enumerate((add_over_x, add_low, amplitude, pass_low, gather_over_x, amps_here)):
        for g in range(chunks):
            schedule[steps[g][at]].append((stage, g))
    for g in range(chunks):
        for j in range(2):
            ready = max(steps[g][5], pieces + 2 * g + j)
            schedule[ready].append((density, 2 * g + j))
    for n in range(2 * pieces + 1):
        if n < 2 * pieces:
            if n < pieces and n % 2 == 0:
                core_copy(n // 2).wait_recv()
            halo_wait_recv(n)
            advance()
            if n < pieces:
                coulomb(n // 2, n % 2)
        stages = list(schedule[n])
        for stage, at in stages[: len(stages) // 2]:
            stage(at)
        advance()
        for stage, at in stages[len(stages) // 2 :]:
            stage(at)

    for j in range(pieces):
        gamma_copy(j).wait_send()
        store(j).wait()
    for j in range(chunks):
        core_copy(j).wait_send()
        low_copy(j).wait_send()
        for d in range(1, X):
            part_copy(j, d).wait_send()
            panel_copy(j, d).wait_send()
        for d in range(1, ZH):
            unit_copy(j, d).wait_send()
            amp_copy(j, d).wait_send()

    @pl.when(zh >= 2)
    def _():
        for j in range(chunks):
            amp_up_copy(j).wait_send()
            for d in range(1, ZH):
                amp_low_copy(j, d).wait_send()

    for j in range(pieces):
        arrived(out_ref.at[pl.ds(other * HALF + j * PIECE, PIECE)], out_recv.at[j], out_send.at[j])


def density(raw, rows, slab_owner, occ_energy, pair_mask, vir_energy):
    slabs = raw.shape[0] // rows
    dma = pltpu.SemaphoreType.DMA
    bf16, f32 = jnp.bfloat16, jnp.float32
    hbm = pl.BlockSpec(memory_space=pltpu.HBM)
    smem = pltpu.SMEM
    chunks, pieces = HALF // CHUNK, HALF // PIECE
    return pl.pallas_call(
        functools.partial(density_kernel, lax.axis_size("occ")),
        out_shape=jax.ShapeDtypeStruct((slabs, rows, LANES), bf16),
        in_specs=[hbm] * 5,
        out_specs=hbm,
        scratch_shapes=[
            smem(slab_owner.shape, slab_owner.dtype),
            smem(occ_energy.shape, f32),
            smem(pair_mask.shape, pair_mask.dtype),
            VMEM(vir_energy.shape, f32),
            VMEM(raw.shape, bf16),
            dma((5,)),
            VMEM((slabs, rows, LANES), bf16),
            VMEM((slabs, rows, LANES), f32),
            VMEM((2, HALF, rows, LANES), bf16),
            VMEM((2, 2, HALF, rows, LANES), bf16),
            VMEM((chunks, X, 3, LANES, LANES), PART),
            VMEM((chunks, X, 3, LANES, LANES), f32),
            VMEM((chunks, X, 3, LANES, LANES), PART),
            VMEM((chunks, ZH, SLAB, LANES), f32),
            VMEM((chunks, 6, SLAB, LANES), PART),
            VMEM((chunks, ZH, SLAB, LANES), PART),
            VMEM((chunks, 2, SLAB, LANES), PART),
            VMEM((HALF, 6, SLAB, LANES), bf16),
            VMEM((HALF, rows, LANES), bf16),
            VMEM((HALF, rows, LANES), bf16),
            dma, dma((chunks,)), dma((chunks,)), dma((2 * pieces, 2)), dma((2 * pieces, 2)),
            dma((chunks, X)), dma((chunks, X)),
            dma((chunks, ZH)), dma((chunks, ZH)), dma((chunks,)), dma((chunks,)),
            dma((chunks, ZH)), dma((chunks, ZH)), dma((chunks,)), dma((chunks,)),
            dma((chunks, ZH)), dma((chunks, ZH)),
            dma((chunks, X)), dma((chunks, X)), dma((pieces,)), dma((pieces,)), dma((pieces,)),
        ],
        compiler_params=pltpu.CompilerParams(
            collective_id=0, has_side_effects=True, vmem_limit_bytes=57 << 20
        ),
        name="density",
    )(slab_owner, occ_energy, pair_mask, vir_energy, raw)


def on_device(b_factors, occ_energy, vir_energy, slab_owner, pair_mask):
    aux_rows, occ_rows, virtuals = b_factors.shape
    tiles = virtuals // LANES
    raw = b_factors.reshape(aux_rows, occ_rows, tiles, LANES)
    raw = jnp.swapaxes(raw, 1, 2).reshape(aux_rows * tiles * occ_rows, LANES)
    gamma = density(
        raw, aux_rows, slab_owner, occ_energy, jnp.swapaxes(pair_mask, 0, 1),
        vir_energy.reshape(tiles, LANES),
    )
    raw = ungroup(gamma).reshape(aux_rows, tiles, occ_rows, LANES)
    return jnp.swapaxes(raw, 1, 2).reshape(aux_rows, occ_rows, virtuals)


def solution(mesh):
    placed = (P("aux", "occ", None), P(), P(), P(), P("occ", None, None))
    return jax.shard_map(
        on_device, mesh=mesh, in_specs=placed, out_specs=P("aux", "occ", None), check_vma=False
    )
```

```python
import functools

import jax
import jax.numpy as jnp
from jax import lax
from jax.experimental import pallas as pl
from jax.experimental.pallas import tpu as pltpu
from jax.sharding import PartitionSpec as P

SLAB = 64
LANES = 128
X, ZH, CORES = 4, 4, 2
HALF = 16
CHUNK = 4
PIECE = 2
FAR_FIRST = (2, 1, 3)
AHEAD = 4
STEP = 16
PART = jnp.bfloat16
MESH = pl.DeviceIdType.MESH
VMEM = pltpu.VMEM


def low_half(shape):
    return lax.broadcasted_iota(jnp.int32, shape, len(shape) - 1) < SLAB


def split_rows(raw_ref, wide):
    @pl.loop(0, wide.shape[1] // STEP)
    def _(n):
        at = pl.multiple_of(n * STEP * 32, STEP * 32)
        block = raw_ref[pl.ds(at, STEP * 32), :].astype(jnp.float32)
        wide[:, pl.ds(pl.multiple_of(n * STEP, STEP), STEP), :] = jnp.swapaxes(
            block.reshape(STEP, 32, LANES), 0, 1
        )


def slab_panel(slab, wide):
    odd = slab % 2
    kept = wide[slab]
    moved = pltpu.roll(wide[slab + 1 - 2 * odd], SLAB, 1)
    lane = lax.broadcasted_iota(jnp.int32, kept.shape, 1)
    return jnp.where(lane // SLAB == odd, kept, moved).astype(jnp.bfloat16)


def ungroup_kernel(gamma_in, out_ref, gamma_ref, raw_ref, load_sem, sem):
    slabs, rows, _ = gamma_ref.shape

    def lay_out(n):
        at = pl.ds(pl.multiple_of(n * STEP, STEP), STEP)
        block = gamma_ref[:, at, :].astype(jnp.float32).reshape(slabs // 2, 2, STEP, LANES)
        even, odd = block[:, 0], block[:, 1]
        left = low_half(even.shape)
        moved = pltpu.roll(jnp.where(left, odd, even), SLAB, 2)
        pairs = jnp.stack([jnp.where(left, even, moved), jnp.where(left, moved, odd)], axis=1)
        lines = jnp.swapaxes(pairs.reshape(slabs, STEP, LANES), 0, 1)
        to = pl.ds(pl.multiple_of(n * STEP * 32, STEP * 32), STEP * 32)
        raw_ref[to, :] = lines.reshape(STEP * 32, LANES).astype(raw_ref.dtype)

    shares = 3
    share = raw_ref.shape[0] // shares
    steps = rows // STEP // shares
    loads, stores = [], []
    for at in range(shares):
        part = pl.ds(at * steps * STEP, steps * STEP)
        loads.append(
            pltpu.make_async_copy(gamma_in.at[:, part], gamma_ref.at[:, part], load_sem.at[at])
        )
        loads[-1].start()
    for at in range(shares):
        loads[at].wait()
        pl.loop(at * steps, (at + 1) * steps)(lay_out)
        done = pl.ds(at * share, share)
        stores.append(pltpu.make_async_copy(raw_ref.at[done], out_ref.at[done], sem.at[at]))
        stores[-1].start()
    for store in stores:
        store.wait()


def ungroup(gamma):
    slabs, rows, _ = gamma.shape
    return pl.pallas_call(
        ungroup_kernel,
        out_shape=jax.ShapeDtypeStruct((slabs * rows, LANES), gamma.dtype),
        in_specs=[pl.BlockSpec(memory_space=pltpu.HBM)],
        out_specs=pl.BlockSpec(memory_space=pltpu.HBM),
        scratch_shapes=[
            VMEM(gamma.shape, gamma.dtype), VMEM((slabs * rows, LANES), gamma.dtype),
            pltpu.SemaphoreType.DMA((3,)), pltpu.SemaphoreType.DMA((3,)),
        ],
        compiler_params=pltpu.CompilerParams(vmem_limit_bytes=57 << 20),
        name="ungroup",
    )(gamma)


def dot(a, b, ca, cb):
    return lax.dot_general(a, b, (((ca,), (cb,)), ((), ())), preferred_element_type=jnp.float32)


def density_kernel(
    occ_count,
    slab_in, occ_in, mask_in, vir_in, raw_in,
    out_ref,
    slab_ref, occ_ref, mask_ref, vir_ref, raw_ref, load_sem,
    own_ref, wide,
    panel, near, part, part_wide, part_in, total, unit_out, unit_in, low_in, amp, gamma_out, gamma_own,
    copy_sem, core_send, core_recv, halo_send, halo_recv, x_send, x_recv,
    z_send, z_recv, low_send, low_recv, za_send, za_recv, up_send, up_recv, zl_send, zl_recv,
    xa_send, xa_recv, out_send, out_recv, store_sem,
):
    o = lax.axis_index("occ")
    aux = lax.axis_index("aux")
    core = aux % CORES
    zh = (aux // CORES) % ZH
    x = aux // (CORES * ZH)
    other = 1 - core

    def device(occ, x_at, z_at, core_at):
        return (occ, (x_at * ZH + z_at) * CORES + core_at)

    below = lax.rem(o + occ_count - 1, occ_count)
    above = lax.rem(o + 1, occ_count)
    x_peers = [lax.rem(x + d, X) for d in range(X)]
    z_peers = [lax.rem(zh + d, ZH) for d in range(ZH)]

    def remote(src, dst, send, recv, to):
        return pltpu.make_async_remote_copy(
            src_ref=src, dst_ref=dst, send_sem=send, recv_sem=recv, device_id=to,
            device_id_type=MESH,
        )

    def arrived(landed, recv, send):
        remote(landed, landed, send, recv, device(above, x, zh, core)).wait_recv()

    partners = [device(o, x, zh, other)]
    partners += [device(b, x, zh, c) for b in (below, above) for c in (0, 1)]
    partners += [device(o, x_peers[d], zh, core) for d in range(1, X)]
    partners += [device(o, x, z_peers[d], core) for d in range(1, ZH)]
    loads = [
        pltpu.make_async_copy(source, landing, load_sem.at[n])
        for n, (source, landing) in enumerate((
            (raw_in, raw_ref), (slab_in, slab_ref), (occ_in, occ_ref), (mask_in, mask_ref),
            (vir_in, vir_ref),
        ))
    ]
    for load in loads:
        load.start()
    barrier = pltpu.get_barrier_semaphore()
    for partner in partners:
        pl.semaphore_signal(barrier, inc=1, device_id=partner, device_id_type=MESH)
    for load in loads:
        load.wait()
    split_rows(raw_ref, wide)

    def regroup(first, last):
        @pl.loop(first, last)
        def _(q):
            for k in (q, HALF + q):
                own_ref[k] = slab_panel(slab_ref[k], wide)

    regroup(0, CHUNK)
    pl.semaphore_wait(barrier, len(partners))

    chunks = HALF // CHUNK

    def slabs_of(core_at, j):
        return own_ref.at[pl.ds(core_at * HALF + j * CHUNK, CHUNK)]

    def core_copy(j):
        return remote(
            slabs_of(other, j), panel.at[core, pl.ds(j * CHUNK, CHUNK)],
            core_send.at[j], core_recv.at[j], device(o, x, zh, other),
        )

    pieces = HALF // PIECE

    def halo_copy(n, core_at):
        phase, j = divmod(n, pieces)
        way = core if phase == 0 else other
        to = jnp.where(way == 0, below, above)
        return remote(
            own_ref.at[pl.ds(core_at * HALF + j * PIECE, PIECE)],
            near.at[way, core, pl.ds(j * PIECE, PIECE)],
            halo_send.at[n, core_at], halo_recv.at[n, way], device(to, x, zh, core_at),
        )

    halos = [(n, core_at) for n in range(2 * pieces) for core_at in (0, 1)]
    finished = []

    def advance():
        at = len(finished)
        if at < len(halos):
            halo_copy(*halos[at]).wait_send()
            finished.append(at)
            if at + AHEAD < len(halos):
                halo_copy(*halos[at + AHEAD]).start()

    def halo_wait_recv(n):
        phase, j = divmod(n, pieces)
        for way in (0, 1):
            source_core = way if phase == 0 else 1 - way
            arrived(near.at[way, source_core, pl.ds(j * PIECE, PIECE)],
                    halo_recv.at[n, way], halo_send.at[n, 0])

    def part_copy(g, d):
        to = x_peers[d]
        return remote(part.at[g, to], part_in.at[g, d], x_send.at[g, d], x_recv.at[g, d],
                      device(o, to, zh, core))

    def coulomb(g, half):
        @pl.loop(half * PIECE, half * PIECE + PIECE)
        def _(s):
            q = g * CHUNK + s
            first, second = panel[0, q], panel[1, q]
            sums = (
                dot(first, first, 0, 0) + dot(second, second, 0, 0),
                dot(first, near[0, 0, q], 0, 0),
                dot(near[1, 1, q], second, 0, 0),
            )
            for m in range(3):
                part_wide[g, s, m] = sums[m]
                part[g, s, m] = sums[m].astype(PART)

        for d in FAR_FIRST:

            @pl.when(x_peers[d] // PIECE == half)
            def _(d=d):
                part_copy(g, d).start()

    def unit_copy(g, d):
        to = z_peers[d]
        return remote(unit_out.at[g, to], unit_in.at[g, d], z_send.at[g, d], z_recv.at[g, d],
                      device(o, x, to, core))

    def unit_start(g, m):
        for d in FAR_FIRST:

            @pl.when(z_peers[d] // 2 == m)
            def _(d=d):
                unit_copy(g, d).start()

    def low_copy(g):
        return remote(unit_out.at[g, pl.ds(4, 2)], low_in.at[g], low_send.at[g], low_recv.at[g],
                      device(below, x, zh, core))

    def add_over_x(g):
        for d in range(1, X):
            part_copy(g, d).wait_recv()
        for m in (2, 0, 1):
            value = part_wide[g, x, m]
            for d in range(1, X):
                value = value + part_in[g, d, m].astype(jnp.float32)
            for i in range(2):
                half = value[i * SLAB : (i + 1) * SLAB]
                if m < 2:
                    total[g, 2 * m + i] = half
                if m != 1:
                    unit_out[g, 2 * m + i] = half.astype(PART)
            if m == 2:
                low_copy(g).start()
        unit_start(g, 0)

    def add_low(g):
        low_copy(g).wait_recv()
        for i in range(2):
            value = total[g, 2 + i] + low_in[g, i].astype(jnp.float32)
            total[g, 2 + i] = value
            unit_out[g, 2 + i] = value.astype(PART)
        unit_start(g, 1)

    def amp_copy(g, d):
        mine = amp.at[g * CHUNK + x, zh]
        return remote(mine, mine, za_send.at[g, d], za_recv.at[g, d], device(o, x, z_peers[d], core))

    def amp_up_copy(g):
        q = g * CHUNK + x
        return remote(amp.at[q, zh], amp.at[q, zh + 2], up_send.at[g], up_recv.at[g],
                      device(above, x, zh, core))

    def amp_low_copy(g, d):
        mine = amp.at[g * CHUNK + x, zh + 2]
        return remote(mine, mine, zl_send.at[g, d], zl_recv.at[g, d], device(o, x, z_peers[d], core))

    def amplitude(g):
        for d in range(1, ZH):
            unit_copy(g, d).wait_recv()
        value = total[g, zh]
        for d in range(1, ZH):
            value = value + unit_in[g, d].astype(jnp.float32)
        turned = jnp.concatenate([value, value], axis=0).T
        left = low_half(value.shape)
        swapped = jnp.where(left, turned[:SLAB], turned[SLAB:])
        slab = slab_ref[core * HALF + g * CHUNK + x]
        line = vir_ref[pl.ds(slab // 2, 1), :]
        take = low_half(line.shape) == ((slab % 2) == 0)
        line = jnp.where(take, line, pltpu.roll(line, SLAB, 1))
        eps_b = jnp.broadcast_to(line, (LANES, LANES))
        block = jnp.where(zh < 2, o, above)
        eps_i = occ_ref[2 * o + zh % 2]
        eps_j = jnp.where(left, occ_ref[2 * block], occ_ref[2 * block + 1])
        denominator = eps_b.T[:SLAB] + eps_b[:SLAB] - eps_i - eps_j
        weight = mask_ref[1 + zh // 2, 0, slab].astype(jnp.float32)
        amp[g * CHUNK + x, zh] = (
            (2.0 * value - swapped) / denominator * weight
        ).astype(amp.dtype)

        @pl.when(zh >= 2)
        def _():
            amp_up_copy(g).start()

        for d in FAR_FIRST:
            amp_copy(g, d).start()

    def pass_low(g):
        @pl.when(zh >= 2)
        def _():
            amp_up_copy(g).wait_recv()
            for d in FAR_FIRST:
                amp_low_copy(g, d).start()

    def panel_copy(g, d):
        mine = amp.at[g * CHUNK + x]
        return remote(mine, mine, xa_send.at[g, d], xa_recv.at[g, d],
                      device(o, x_peers[d], zh, core))

    def gather_over_x(g):
        q = g * CHUNK + x
        for d in range(1, ZH):
            arrived(amp.at[q, z_peers[ZH - d]], za_recv.at[g, d], za_send.at[g, d])

            @pl.when(z_peers[ZH - d] >= 2)
            def _(d=d):
                arrived(amp.at[q, z_peers[ZH - d] + 2], zl_recv.at[g, d], zl_send.at[g, d])

        for d in FAR_FIRST:
            panel_copy(g, d).start()

    def gamma_copy(j):
        return remote(
            gamma_out.at[pl.ds(j * PIECE, PIECE)],
            out_ref.at[pl.ds(core * HALF + j * PIECE, PIECE)],
            out_send.at[j], out_recv.at[j], device(o, x, zh, other),
        )

    def store(j):
        return pltpu.make_async_copy(
            gamma_own.at[pl.ds(j * PIECE, PIECE)],
            out_ref.at[pl.ds(core * HALF + j * PIECE, PIECE)], store_sem.at[j],
        )

    def amps_here(g):
        for d in range(1, X):
            arrived(amp.at[g * CHUNK + x_peers[X - d]], xa_recv.at[g, d], xa_send.at[g, d])

    def density(j):
        @pl.loop(0, PIECE)
        def _(s):
            q = j * PIECE + s
            own, up, low = (
                amp[q, 2 * m : 2 * m + 2].reshape(LANES, LANES) for m in range(3)
            )

            def rows(at):
                value = dot(panel[at, q], own, 1, 1) + dot(near[0, at, q], up, 1, 1)
                return (value + dot(near[1, at, q], low, 1, 0)).astype(out_ref.dtype)

            gamma_out[q] = rows(other)
            gamma_own[q] = rows(core)

        gamma_copy(j).start()
        store(j).start()

    local = pltpu.make_async_copy(
        own_ref.at[pl.ds(core * HALF, HALF)], panel.at[core], copy_sem
    )
    for at in range(AHEAD):
        halo_copy(*halos[at]).start()
    core_copy(0).start()
    regroup(CHUNK, HALF)
    local.start()
    for j in range(1, chunks):
        core_copy(j).start()
    local.wait()

    steps = ((2, 3, 4, 5, 6, 8), (4, 5, 6, 7, 8, 10), (6, 7, 8, 9, 10, 12), (8, 9, 10, 11, 12, 14))
    schedule = {n: [] for n in range(2 * pieces + 1)}
    for at, stage in enumerate((add_over_x, add_low, amplitude, pass_low, gather_over_x, amps_here)):
        for g in range(chunks):
            schedule[steps[g][at]].append((stage, g))
    for g in range(chunks):
        for j in range(2):
            ready = max(steps[g][5], pieces + 2 * g + j)
            schedule[ready].append((density, 2 * g + j))
    for n in range(2 * pieces + 1):
        if n < 2 * pieces:
            if n < pieces and n % 2 == 0:
                core_copy(n // 2).wait_recv()
            halo_wait_recv(n)
            advance()
            if n < pieces:
                coulomb(n // 2, n % 2)
        stages = list(schedule[n])
        for stage, at in stages[: len(stages) // 2]:
            stage(at)
        advance()
        for stage, at in stages[len(stages) // 2 :]:
            stage(at)

    for j in range(pieces):
        gamma_copy(j).wait_send()
        store(j).wait()
    for j in range(chunks):
        core_copy(j).wait_send()
        low_copy(j).wait_send()
        for d in range(1, X):
            part_copy(j, d).wait_send()
            panel_copy(j, d).wait_send()
        for d in range(1, ZH):
            unit_copy(j, d).wait_send()
            amp_copy(j, d).wait_send()

    @pl.when(zh >= 2)
    def _():
        for j in range(chunks):
            amp_up_copy(j).wait_send()
            for d in range(1, ZH):
                amp_low_copy(j, d).wait_send()

    for j in range(pieces):
        arrived(out_ref.at[pl.ds(other * HALF + j * PIECE, PIECE)], out_recv.at[j], out_send.at[j])


def density(raw, rows, slab_owner, occ_energy, pair_mask, vir_energy):
    slabs = raw.shape[0] // rows
    dma = pltpu.SemaphoreType.DMA
    bf16, f32 = jnp.bfloat16, jnp.float32
    hbm = pl.BlockSpec(memory_space=pltpu.HBM)
    smem = pltpu.SMEM
    chunks, pieces = HALF // CHUNK, HALF // PIECE
    return pl.pallas_call(
        functools.partial(density_kernel, lax.axis_size("occ")),
        out_shape=jax.ShapeDtypeStruct((slabs, rows, LANES), bf16),
        in_specs=[hbm] * 5,
        out_specs=hbm,
        scratch_shapes=[
            smem(slab_owner.shape, slab_owner.dtype),
            smem(occ_energy.shape, f32),
            smem(pair_mask.shape, pair_mask.dtype),
            VMEM(vir_energy.shape, f32),
            VMEM(raw.shape, bf16),
            dma((5,)),
            VMEM((slabs, rows, LANES), bf16),
            VMEM((slabs, rows, LANES), f32),
            VMEM((2, HALF, rows, LANES), bf16),
            VMEM((2, 2, HALF, rows, LANES), bf16),
            VMEM((chunks, X, 3, LANES, LANES), PART),
            VMEM((chunks, X, 3, LANES, LANES), f32),
            VMEM((chunks, X, 3, LANES, LANES), PART),
            VMEM((chunks, ZH, SLAB, LANES), f32),
            VMEM((chunks, 6, SLAB, LANES), PART),
            VMEM((chunks, ZH, SLAB, LANES), PART),
            VMEM((chunks, 2, SLAB, LANES), PART),
            VMEM((HALF, 6, SLAB, LANES), bf16),
            VMEM((HALF, rows, LANES), bf16),
            VMEM((HALF, rows, LANES), bf16),
            dma, dma((chunks,)), dma((chunks,)), dma((2 * pieces, 2)), dma((2 * pieces, 2)),
            dma((chunks, X)), dma((chunks, X)),
            dma((chunks, ZH)), dma((chunks, ZH)), dma((chunks,)), dma((chunks,)),
            dma((chunks, ZH)), dma((chunks, ZH)), dma((chunks,)), dma((chunks,)),
            dma((chunks, ZH)), dma((chunks, ZH)),
            dma((chunks, X)), dma((chunks, X)), dma((pieces,)), dma((pieces,)), dma((pieces,)),
        ],
        compiler_params=pltpu.CompilerParams(
            collective_id=0, has_side_effects=True, vmem_limit_bytes=57 << 20
        ),
        name="density",
    )(slab_owner, occ_energy, pair_mask, vir_energy, raw)


def on_device(b_factors, occ_energy, vir_energy, slab_owner, pair_mask):
    aux_rows, occ_rows, virtuals = b_factors.shape
    tiles = virtuals // LANES
    raw = b_factors.reshape(aux_rows, occ_rows, tiles, LANES)
    raw = jnp.swapaxes(raw, 1, 2).reshape(aux_rows * tiles * occ_rows, LANES)
    gamma = density(
        raw, aux_rows, slab_owner, occ_energy, jnp.swapaxes(pair_mask, 0, 1),
        vir_energy.reshape(tiles, LANES),
    )
    raw = ungroup(gamma).reshape(aux_rows, tiles, occ_rows, LANES)
    return jnp.swapaxes(raw, 1, 2).reshape(aux_rows, occ_rows, virtuals)


def solution(mesh):
    placed = (P("aux", "occ", None), P(), P(), P(), P("occ", None, None))
    return jax.shard_map(
        on_device, mesh=mesh, in_specs=placed, out_specs=P("aux", "occ", None), check_vma=False
    )
```
